32 devices in a mesh: rows: 8 (over z, x), table: 4 (over y, core).
Axes of the slice: x: 2, y: 2, z: 4, core: 2. Of those that a mesh axis runs over, the one named last changes fastest.
Arguments:
- item_table: bfloat16 [524288, 128], P(('rows', 'table')), may hold values from -40 to 40, as said below
- user_rows: float32 [2048, 128], P(('rows', 'table')), may hold values from -3 to 3
- link_rows: int32 [2048, 128], P(('rows', 'table')), may hold values from 0 to 16383
- link_slots: int32 [2048, 128], P(('rows', 'table')), may hold values from 0 to 8191, as said below
- link_weights: int32 [2048, 128], P(('rows', 'table')), may hold values from 1 to 63
- link_counts: int32 [2048], P(('rows', 'table')), may hold values from 1 to 128
Outputs:
- solved_rows: float32 [2048, 128], P(('rows', 'table'))
The draws below stay inside these ranges and needn't reach their ends.
Inputs may be any that keep to these rules, and one draw needn't show every extreme that they name: `item_table`: rows differ in scale; values lie within the stated bounds. `link_slots`: on each device (flat index over rows then table, users in blocks of 64), its 8192 entries hold every number of 0 to 8191 exactly once; entry s names slot s % 256 toward the device of flat index s // 256, which holds the linked item, so every device names exactly 256 slots of every owner, live or not.
All inputs are finite; a program needn't handle non-finite values.
Results may differ from the reference program's by a relative error of at most 0.0019.
Values may be sent and summed in bfloat16 or wider, within the bound.
A program may use at most 64 MiB of HBM per device.

```python
import math
import jax
import jax.numpy as jnp
import numpy as np
from jax import lax

K = 128
L = 128
CG_STEPS = 3
U_DEV = 64
ITEM_DEV = 16384
USERS = 2048
ITEMS = 524288
CAP = 256
N_ROWS = 8
N_TABLE = 4


def draw_item_table(key, part):
    key = jax.random.fold_in(key, 11)
    key_noise, key_scale, key_center = jax.random.split(key, 3)
    ramp = (jnp.arange(ITEMS) // ITEM_DEV).astype(jnp.float32) / max(ITEMS // ITEM_DEV - 1, 1)
    noise = jnp.clip(jax.random.normal(key_noise, (ITEMS, K), jnp.float32), -4.0, 4.0)
    row_scale = 0.3 * jnp.exp(jax.random.uniform(key_scale, (ITEMS, 1), jnp.float32) * jnp.log(10.0))
    center = jax.random.uniform(key_center, (1, K), jnp.float32, -1.0, 1.0)
    ramp_scale = jnp.exp(ramp * 0.5 * jnp.log(3.0))
    return ((noise + center) * row_scale * ramp_scale[:, None]).astype(jnp.bfloat16)


def draw_link_slots(key, part):
    key = jax.random.fold_in(key, 23)
    device_keys = jax.random.split(key, ITEMS // ITEM_DEV)
    orders = jax.vmap(lambda single: jax.random.permutation(single, U_DEV * L))(device_keys)
    return orders.reshape(USERS, L).astype(jnp.int32)


def place_ends(result, stream_key, least, top_value):
    place = [jax.random.randint(jax.random.fold_in(stream_key, axis), (), 0, length) for axis, length in enumerate(result.shape)]
    main_axis = result.shape.index(max(result.shape))
    neighbour = place[:main_axis] + [(place[main_axis] + 1) % result.shape[main_axis]] + place[main_axis + 1:]
    return result.at[tuple(place)].set(least).at[tuple(neighbour)].set(top_value)


def block_levels(rng, extent, cuts, smallest, largest):
    gain, own = 1.0, jax.random.fold_in(rng, 6)
    for axis_at, parts in cuts:
        draws = jnp.exp(jax.random.uniform(jax.random.fold_in(own, axis_at), (parts,), jnp.float32, smallest / len(cuts), largest / len(cuts)))
        gain = gain * jnp.repeat(draws, extent[axis_at] // parts).reshape([-1 if axis == axis_at else 1 for axis in range(len(extent))])
    return gain


def cumulative_ranks(amount, slope):
    weights = [(1 << 20) // math.isqrt(rank ** slope) + 1 for rank in range(1, amount + 1)]
    spread = 1 + sum(weights) // (1 << 30)
    return np.cumsum(np.array([max(1, weight // spread) for weight in weights]))


def ranked_ids(key, shape, count, slope):
    table = cumulative_ranks(count, slope)
    lot = jax.random.randint(jax.random.fold_in(key, 1), shape, 0, int(table[count - 1]))
    rank = jnp.searchsorted(jnp.asarray(table, jnp.int32), lot, side="right")
    return jax.random.permutation(jax.random.fold_in(key, 2), count)[rank].astype(jnp.int32)


def gaussian(key, shape, width, reach, cuts=(), kind=jnp.bfloat16):
    entries = width * jax.random.normal(key, shape, jnp.float32)
    if cuts:
        entries = entries * block_levels(key, shape, cuts, -0.22, 0.18)
    return jnp.clip(entries, -reach, reach).astype(kind)


def setup_inputs(seed: int = 0) -> dict:
    keys = jax.random.split(jax.random.key(seed), 7)
    item_table = draw_item_table(jax.random.fold_in(keys[6], 71), 0)
    user_rows = gaussian(keys[1], (USERS, K), 0.5, 3.0, ((0, 32),), jnp.float32)
    link_rows = place_ends(ranked_ids(keys[2], (USERS, L), ITEM_DEV, 2), jax.random.fold_in(keys[2], 3), 0, ITEM_DEV - 1).astype(jnp.int32)
    link_slots = draw_link_slots(jax.random.fold_in(keys[6], 71), 0)
    link_weights = place_ends(jax.random.randint(keys[4], (USERS, L), 1, 64), jax.random.fold_in(keys[4], 1), 1, 63).astype(jnp.int32)
    link_counts = place_ends(jax.random.randint(keys[5], (USERS,), 1, L + 1), jax.random.fold_in(keys[5], 1), 1, L).astype(jnp.int32)
    return {"item_table": item_table, "user_rows": user_rows, "link_rows": link_rows, "link_slots": link_slots, "link_weights": link_weights, "link_counts": link_counts}


def refine(apply_system, target, initial):
    estimate = initial
    residual = target - apply_system(estimate)
    direction = residual
    norm_now = jnp.sum(residual * residual, axis=1, keepdims=True)
    for iteration in range(CG_STEPS):
        image = apply_system(direction)
        curvature = jnp.sum(direction * image, axis=1, keepdims=True)
        step_len = norm_now / (curvature + 1e-6)
        estimate = estimate + step_len * direction
        residual = residual - step_len * image
        norm_next = jnp.sum(residual * residual, axis=1, keepdims=True)
        direction = residual + (norm_next / (norm_now + 1e-6)) * direction
        norm_now = norm_next
    return estimate


def reference(item_table, user_rows, link_rows, link_slots, link_weights, link_counts):
    device_count = N_ROWS * N_TABLE
    gramian = jnp.dot(item_table.T, item_table, preferred_element_type=jnp.float32)
    shared = gramian * (L / ITEMS) + (0.5 * L) * jnp.eye(K, dtype=jnp.float32)
    owners = (link_slots // CAP).astype(jnp.int32)
    item_ids = (owners * ITEM_DEV + link_rows).astype(jnp.int32)

    def solve_block(pieces):
        ids_block, weight_block, count_block, start_block = pieces
        fetched = item_table[ids_block]
        live_mask = jnp.arange(L, dtype=jnp.int32)[None, :] < count_block[:, None]
        confidence = jnp.where(live_mask, 1.0 + weight_block.astype(jnp.float32) / 8.0, 0.0).astype(jnp.float32)
        scaled = (confidence[:, :, None] * fetched.astype(jnp.float32)).astype(jnp.bfloat16)
        weighted = jnp.einsum("ulk,ulm->ukm", scaled.astype(jnp.float32), fetched.astype(jnp.float32), precision=lax.Precision.HIGHEST)
        system = shared[None, :, :] + weighted
        target = jnp.sum(scaled.astype(jnp.float32), axis=1)

        def apply_system(vector):
            return jnp.einsum("ukm,um->uk", system, vector, precision=lax.Precision.HIGHEST)

        return refine(apply_system, target, start_block)

    solved = lax.map(solve_block, (item_ids.reshape(device_count, U_DEV, L), link_weights.reshape(device_count, U_DEV, L), link_counts.reshape(device_count, U_DEV), user_rows.reshape(device_count, U_DEV, K)))
    return solved.reshape(USERS, K)
```

```python
import functools

import jax
import jax.numpy as jnp
from jax import lax
from jax.experimental import pallas as pl
from jax.experimental.pallas import tpu as pltpu
from jax.sharding import PartitionSpec as P

CG_STEPS = 3
MESH = pl.DeviceIdType.MESH
VMEM_BYTES = 50 * 1024 * 1024
NT = (((1,), (1,)), ((), ()))
TN = (((0,), (0,)), ((), ()))


def position():
    width = lax.axis_size("table")
    count = lax.axis_size("rows") * width
    return lax.axis_index("rows") * width + lax.axis_index("table"), count, width


def partner(step):
    me, count, width = position()
    other = lax.rem(me + step, count)
    return other, (other // width, lax.rem(other, width))


def greet_all():
    _, count, _ = position()
    barrier = pltpu.get_barrier_semaphore()

    def greet(step, carry):
        pl.semaphore_signal(barrier, inc=1, device_id=partner(step)[1], device_id_type=MESH)
        return carry

    lax.fori_loop(1, count, greet, 0)
    pl.semaphore_wait(barrier, count - 1)


def for_partners(body):
    _, count, _ = position()

    def step_body(step, carry):
        body(*partner(step))
        return carry

    lax.fori_loop(1, count, step_body, 0)


def place_requests(slots_ref, rows_ref, owners, capacity):
    users, width = slots_ref.shape
    shift = capacity.bit_length() - 1
    group = 8

    def one_group(index, total):
        at = pl.ds(pl.multiple_of(index * group, group), group)
        slots, rows = slots_ref[at, :], rows_ref[at, :]
        owner, inner = slots >> shift, slots & (capacity - 1)
        high, low = (rows >> 7).astype(jnp.float32), (rows & 127).astype(jnp.float32)
        for user in range(group):
            pick = slice(user, user + 1)
            match = lax.broadcasted_iota(jnp.int32, (owners, width), 0) == owner[pick]
            left = jnp.concatenate(
                [jnp.where(match, high[pick], 0.0), jnp.where(match, low[pick], 0.0)], axis=0
            ).astype(jnp.bfloat16)
            hit = lax.broadcasted_iota(jnp.int32, (capacity, width), 0) == inner[pick]
            right = jnp.where(hit, 1.0, 0.0).astype(jnp.bfloat16)
            total = total + lax.dot_general(left, right, NT, preferred_element_type=jnp.float32)
        return total

    total = lax.fori_loop(
        0, users // group, one_group, jnp.zeros((2 * owners, capacity), jnp.float32)
    )
    return (total[:owners] * 128.0 + total[owners:]).astype(jnp.int32)


def request_kernel(slots_ref, rows_ref, asked_ref, wanted, send_sem, recv_sem):
    me, count, _ = position()
    capacity = wanted.shape[2]
    wanted[...] = place_requests(slots_ref, rows_ref, count, capacity)[:, None, :]
    greet_all()

    def copy(other, device):
        return pltpu.make_async_remote_copy(
            src_ref=wanted.at[other], dst_ref=asked_ref.at[me],
            send_sem=send_sem.at[other], recv_sem=recv_sem.at[me],
            device_id=device, device_id_type=MESH,
        )

    def landing(other, device):
        return pltpu.make_async_remote_copy(
            src_ref=wanted.at[other], dst_ref=asked_ref.at[other],
            send_sem=send_sem.at[other], recv_sem=recv_sem.at[other],
            device_id=device, device_id_type=MESH,
        )

    for_partners(lambda other, device: copy(other, device).start())
    asked_ref[me] = wanted[me]
    for_partners(lambda other, device: landing(other, device).wait())


def table_pass(table_ref, wide, features):
    chunk = 1024

    def one_chunk(index, total):
        at = pl.ds(pl.multiple_of(index * chunk, chunk), chunk)
        block = table_ref[at, :]
        wide[at, :] = block.astype(jnp.float32)
        return total + lax.dot_general(block, block, TN, preferred_element_type=jnp.float32)

    return lax.fori_loop(
        0, table_ref.shape[0] // chunk, one_chunk, jnp.zeros((features, features), jnp.float32)
    )


def gather_rows(read_index, source, target, base, amount):
    group = 32

    def one_group(index, carry):
        start = index * group
        values = [source[pl.ds(read_index(start + i), 1), :] for i in range(group)]
        for i, value in enumerate(values):
            target[pl.ds(base + start + i, 1), :] = value
        return carry

    lax.fori_loop(0, amount // group, one_group, 0)


def gather_kernel(asked_ref, table_ref, rows_ref, gram_ref, wide, stage):
    owners, _, capacity = asked_ref.shape
    features = table_ref.shape[1]
    share = features // owners
    gram = table_pass(table_ref, wide, features)
    for index in range(owners):
        gram_ref[index] = gram[index * share:(index + 1) * share]

    def one_block(other, carry):
        gather_rows(lambda i: asked_ref[other, 0, i], wide, stage, 0, capacity)
        at = pl.ds(pl.multiple_of(other * capacity, capacity), capacity)
        rows_ref[at, :] = stage[...].astype(jnp.bfloat16)
        return carry

    lax.fori_loop(0, owners, one_block, 0)


def exchange_kernel(
    rows_ref, gram_ref, arrived_ref, whole_ref, partial, summed, sems, part_sems, whole_sems
):
    me, count, _ = position()
    capacity = rows_ref.shape[0] // count
    greet_all()

    def block(index):
        return pl.ds(pl.multiple_of(index * capacity, capacity), capacity)

    def part_copy(other, device, slot):
        return pltpu.make_async_remote_copy(
            src_ref=gram_ref.at[other], dst_ref=partial.at[slot],
            send_sem=part_sems.at[0, other], recv_sem=part_sems.at[1, slot],
            device_id=device, device_id_type=MESH,
        )

    def whole_copy(other, device, slot):
        return pltpu.make_async_remote_copy(
            src_ref=summed, dst_ref=whole_ref.at[slot],
            send_sem=whole_sems.at[0, other], recv_sem=whole_sems.at[1, slot],
            device_id=device, device_id_type=MESH,
        )

    def rows_copy(other, device, slot):
        return pltpu.make_async_remote_copy(
            src_ref=rows_ref.at[block(other)], dst_ref=arrived_ref.at[block(slot)],
            send_sem=sems.at[0, other], recv_sem=sems.at[1, slot],
            device_id=device, device_id_type=MESH,
        )

    for_partners(lambda other, device: part_copy(other, device, me).start())
    for_partners(lambda other, device: rows_copy(other, device, me).start())
    partial[me] = gram_ref[me]
    arrived_ref[block(me), :] = rows_ref[block(me), :]
    for_partners(lambda other, device: part_copy(other, device, other).wait())
    summed[...] = jnp.sum(partial[...], axis=0)
    for_partners(lambda other, device: whole_copy(other, device, me).start())
    whole_ref[me] = summed[...]
    for_partners(lambda other, device: rows_copy(other, device, other).wait())
    for_partners(lambda other, device: whole_copy(other, device, other).wait())


def solve_kernel(
    total_items,
    slots_ref, counts_ref, arrived_ref, gram_ref, weights_ref, start_ref, out_ref,
    wide, fetched, scaled, shared, target, vector, image,
):
    users, features = start_ref.shape
    slot_count = weights_ref.shape[1]
    owners, share, _ = gram_ref.shape
    group = 8
    for index in range(owners):
        shared[index * share:(index + 1) * share, :] = gram_ref[index]
    line = lax.broadcasted_iota(jnp.int32, (features, features), 0)
    column = lax.broadcasted_iota(jnp.int32, (features, features), 1)
    shared[...] = shared[...] * (slot_count / total_items) + jnp.where(
        line == column, 0.5 * slot_count, 0.0
    )
    wide[...] = arrived_ref[...].astype(jnp.float32)

    def fetch_user(user, carry):
        base = user * slot_count
        gather_rows(lambda i: slots_ref[user, i], wide, fetched, base, slot_count)
        return carry

    lax.fori_loop(0, users, fetch_user, 0)

    def rows_of(user):
        return pl.ds(pl.multiple_of(user * slot_count, slot_count), slot_count)

    def group_at(index):
        return pl.ds(pl.multiple_of(index * group, group), group)

    def scale_group(index, carry):
        at = group_at(index)
        place = lax.broadcasted_iota(jnp.int32, (group, slot_count), 0)
        limit = jnp.zeros((group, slot_count), jnp.int32)
        for j in range(group):
            limit = jnp.where(place == j, counts_ref[index * group + j], limit)
        live = lax.broadcasted_iota(jnp.int32, (group, slot_count), 1) < limit
        confidence = jnp.where(live, 1.0 + weights_ref[at, :].astype(jnp.float32) / 8.0, 0.0)
        turned = confidence.T
        sums = []
        for j in range(group):
            rows = rows_of(index * group + j)
            product = (turned[:, j:j + 1] * fetched[rows, :]).astype(jnp.bfloat16)
            product = product.astype(jnp.float32)
            scaled[rows, :] = product
            sums.append(jnp.sum(product, axis=0, keepdims=True))
        target[at, :] = jnp.concatenate(sums, axis=0)
        return carry

    lax.fori_loop(0, users // group, scale_group, 0)

    def apply_system(value):
        vector[...] = value

        def apply_group(index, carry):
            at = group_at(index)
            some = vector[at, :]
            images = []
            for j in range(group):
                rows = rows_of(index * group + j)
                inner = jnp.sum(fetched[rows, :] * some[j:j + 1], axis=1, keepdims=True)
                images.append(jnp.sum(scaled[rows, :] * inner, axis=0, keepdims=True))
            image[at, :] = jnp.concatenate(images, axis=0)
            return carry

        lax.fori_loop(0, users // group, apply_group, 0)
        common = lax.dot_general(
            value, shared[...], NT,
            precision=lax.Precision.HIGHEST, preferred_element_type=jnp.float32,
        )
        return common + image[...]

    estimate = start_ref[...]
    residual = target[...] - apply_system(estimate)
    direction = residual
    norm_now = jnp.sum(residual * residual, axis=1, keepdims=True)
    for _ in range(CG_STEPS):
        moved = apply_system(direction)
        curvature = jnp.sum(direction * moved, axis=1, keepdims=True)
        step_len = norm_now / (curvature + 1e-06)
        estimate = estimate + step_len * direction
        residual = residual - step_len * moved
        norm_next = jnp.sum(residual * residual, axis=1, keepdims=True)
        direction = residual + norm_next / (norm_now + 1e-06) * direction
        norm_now = norm_next
    out_ref[...] = estimate


def per_device(item_table, user_rows, link_rows, link_slots, link_weights, link_counts):
    user_count, features = user_rows.shape
    slot_count = link_rows.shape[1]
    devices = lax.axis_size("rows") * lax.axis_size("table")
    link_total = user_count * slot_count
    capacity = link_total // devices
    share = features // devices
    total_items = item_table.shape[0] * devices
    vmem = pl.BlockSpec(memory_space=pltpu.VMEM)
    smem = pl.BlockSpec(memory_space=pltpu.SMEM)
    dma = pltpu.SemaphoreType.DMA
    f32 = jnp.float32

    asked = pl.pallas_call(
        request_kernel,
        out_shape=jax.ShapeDtypeStruct((devices, 1, capacity), jnp.int32),
        in_specs=[vmem, vmem],
        out_specs=vmem,
        scratch_shapes=[
            pltpu.VMEM((devices, 1, capacity), jnp.int32), dma((devices,)), dma((devices,)),
        ],
        compiler_params=pltpu.CompilerParams(
            collective_id=0, has_side_effects=True, vmem_limit_bytes=VMEM_BYTES
        ),
        name="place_and_ask",
    )(link_slots, link_rows)

    rows, gram = pl.pallas_call(
        gather_kernel,
        out_shape=[
            jax.ShapeDtypeStruct((link_total, features), jnp.bfloat16),
            jax.ShapeDtypeStruct((devices, share, features), f32),
        ],
        in_specs=[smem, vmem],
        out_specs=[vmem, vmem],
        scratch_shapes=[
            pltpu.VMEM(item_table.shape, f32), pltpu.VMEM((capacity, features), f32),
        ],
        compiler_params=pltpu.CompilerParams(vmem_limit_bytes=VMEM_BYTES),
        name="gather_and_gramian",
    )(asked, item_table)

    arrived, whole = pl.pallas_call(
        exchange_kernel,
        out_shape=[
            jax.ShapeDtypeStruct((link_total, features), jnp.bfloat16),
            jax.ShapeDtypeStruct((devices, share, features), f32),
        ],
        in_specs=[vmem, vmem],
        out_specs=[vmem, vmem],
        scratch_shapes=[
            pltpu.VMEM((devices, share, features), f32), pltpu.VMEM((share, features), f32),
            dma((2, devices)), dma((2, devices)), dma((2, devices)),
        ],
        compiler_params=pltpu.CompilerParams(
            collective_id=1, has_side_effects=True, vmem_limit_bytes=VMEM_BYTES
        ),
        name="exchange_rows",
    )(rows, gram)

    return pl.pallas_call(
        functools.partial(solve_kernel, total_items),
        out_shape=jax.ShapeDtypeStruct((user_count, features), f32),
        in_specs=[smem, smem, vmem, vmem, vmem, vmem],
        out_specs=vmem,
        scratch_shapes=[
            pltpu.VMEM((link_total, features), f32),
            pltpu.VMEM((link_total, features), f32),
            pltpu.VMEM((link_total, features), f32),
            pltpu.VMEM((features, features), f32),
            pltpu.VMEM((user_count, features), f32),
            pltpu.VMEM((user_count, features), f32),
            pltpu.VMEM((user_count, features), f32),
        ],
        compiler_params=pltpu.CompilerParams(vmem_limit_bytes=VMEM_BYTES),
        name="reorder_and_solve",
    )(link_slots, link_counts, arrived, whole, link_weights, user_rows)


def solution(mesh):
    flat = P(("rows", "table"), None)
    return jax.shard_map(
        per_device,
        mesh=mesh,
        in_specs=(flat, flat, flat, flat, flat, P(("rows", "table"))),
        out_specs=flat,
        check_vma=False,
    )
```

```python
import functools

import jax
import jax.numpy as jnp
from jax import lax
from jax.experimental import pallas as pl
from jax.experimental.pallas import tpu as pltpu
from jax.sharding import PartitionSpec as P

CG_STEPS = 3
MESH = pl.DeviceIdType.MESH
VMEM_BYTES = 50 * 1024 * 1024
NT = (((1,), (1,)), ((), ()))
TN = (((0,), (0,)), ((), ()))


def position():
    width = lax.axis_size("table")
    count = lax.axis_size("rows") * width
    return lax.axis_index("rows") * width + lax.axis_index("table"), count, width


def partner(step):
    me, count, width = position()
    away = count // 2 + (1 - 2 * lax.rem(step, 2)) * ((step + 1) // 2)
    later, earlier = lax.rem(me + away, count), lax.rem(me - away + count, count)
    return later, earlier, (later // width, lax.rem(later, width))


def for_partners(body, first=0, last=None):
    _, count, _ = position()

    def step_body(step, carry):
        body(*partner(step))
        return carry

    lax.fori_loop(first, count - 1 if last is None else last, step_body, 0)


def split(value):
    high = value.astype(jnp.bfloat16)
    low = (value - high.astype(jnp.float32)).astype(jnp.bfloat16)
    return jnp.concatenate([high, low], axis=0)


def joined(value):
    half = value.shape[0] // 2
    return value[:half] + value[half:]


def place_links(slots_ref, rows_ref, weights_ref, counts_ref, owners, capacity):
    users, width = slots_ref.shape
    shift = capacity.bit_length() - 1
    group = 8

    def one_group(index, total):
        at = pl.ds(pl.multiple_of(index * group, group), group)
        slots, rows = slots_ref[at, :], rows_ref[at, :]
        owner, inner = slots >> shift, slots & (capacity - 1)
        high, low = (rows >> 7).astype(jnp.float32), (rows & 127).astype(jnp.float32)
        line = lax.broadcasted_iota(jnp.int32, (group, width), 0)
        limit = jnp.zeros((group, width), jnp.int32)
        for j in range(group):
            limit = jnp.where(line == j, counts_ref[index * group + j], limit)
        live = lax.broadcasted_iota(jnp.int32, (group, width), 1) < limit
        confidence = jnp.where(live, 1.0 + weights_ref[at, :].astype(jnp.float32) / 8.0, 0.0)
        member = (line + index * group).astype(jnp.float32)
        for user in range(group):
            pick = slice(user, user + 1)
            match = lax.broadcasted_iota(jnp.int32, (owners, width), 0) == owner[pick]
            left = jnp.concatenate(
                [jnp.where(match, part[pick], 0.0) for part in (high, low, member, confidence)],
                axis=0,
            ).astype(jnp.bfloat16)
            hit = lax.broadcasted_iota(jnp.int32, (capacity, width), 0) == inner[pick]
            right = jnp.where(hit, 1.0, 0.0).astype(jnp.bfloat16)
            total = total + lax.dot_general(left, right, NT, preferred_element_type=jnp.float32)
        return total

    total = lax.fori_loop(
        0, users // group, one_group, jnp.zeros((4 * owners, capacity), jnp.float32)
    )
    high, low, member, confidence = (total[i * owners:(i + 1) * owners] for i in range(4))
    return (high * 128.0 + low).astype(jnp.int32), member, confidence


def gather_rows(read_index, source, target):
    group = 32

    def one_group(index, carry):
        start = index * group
        values = [source[pl.ds(read_index(start + i), 1), :] for i in range(group)]
        for i, value in enumerate(values):
            target[pl.ds(start + i, 1), :] = value
        return carry

    lax.fori_loop(0, target.shape[0] // group, one_group, 0)


def sweep_kernel(
    total_items,
    counts_ref, table_ref, slots_ref, rows_ref, weights_ref, start_ref, out_ref,
    table, wide, wanted, asked, indices, placed, marks, stage, leaving, arrived, scaled,
    parts, partial, summed, whole, shared, image, target,
    table_sem, index_sem, ask_sems, row_sems, part_sems, whole_sems,
):
    me, count, _ = position()
    users, features = start_ref.shape
    slot_count = slots_ref.shape[1]
    capacity = wanted.shape[2]
    share = features // count
    assert wide.shape[0] & (wide.shape[0] - 1) == 0
    f32 = jnp.float32

    def remote(source, landing, sems, outgoing, incoming, device):
        return pltpu.make_async_remote_copy(
            src_ref=source, dst_ref=landing,
            send_sem=sems.at[0, outgoing], recv_sem=sems.at[1, incoming],
            device_id=device, device_id_type=MESH,
        )

    def ask_copy(to, slot, device):
        return remote(wanted.at[to], asked.at[slot], ask_sems, to, slot, device)

    def row_copy(to, slot, device):
        return remote(leaving.at[to], arrived.at[slot], row_sems, to, slot, device)

    def part_copy(to, slot, device):
        return remote(parts.at[to], partial.at[slot], part_sems, to, slot, device)

    def whole_copy(to, slot, device):
        return remote(summed, whole.at[slot], whole_sems, to, slot, device)

    def finish(copy):
        def both(to, source, device):
            copy(to, source, device).wait()

        return both

    load_table = pltpu.make_async_copy(table_ref, table, table_sem)
    load_table.start()
    barrier = pltpu.get_barrier_semaphore()
    for_partners(
        lambda to, source, device: pl.semaphore_signal(
            barrier, inc=1, device_id=device, device_id_type=MESH
        )
    )
    rows, member, confidence = place_links(
        slots_ref, rows_ref, weights_ref, counts_ref, count, capacity
    )
    wanted[...] = rows[:, None, :]
    placed[0] = member[:, None, :]
    placed[1] = confidence[:, None, :]
    pl.semaphore_wait(barrier, count - 1)
    for_partners(lambda to, source, device: ask_copy(to, me, device).start())
    asked[me] = wanted[me]

    def mark(owner, carry):
        line = lax.broadcasted_iota(jnp.int32, (users, capacity), 0)
        hit = line == placed[0, owner].astype(jnp.int32)
        marks[owner] = jnp.where(hit, placed[1, owner], 0.0)
        return carry

    lax.fori_loop(0, count, mark, 0)

    chunk = 1024
    load_table.wait()

    def widen(index, carry):
        at = pl.ds(pl.multiple_of(index * chunk, chunk), chunk)
        wide[at, :] = table[at, :].astype(f32)
        return carry

    lax.fori_loop(0, table.shape[0] // chunk, widen, 0)

    for_partners(finish(ask_copy))
    load_indices = pltpu.make_async_copy(asked, indices, index_sem)
    load_indices.start()
    load_indices.wait()

    def gather_block(owner):
        gather_rows(lambda i: indices[owner, 0, i] & (wide.shape[0] - 1), wide, stage)
        return stage[...].astype(jnp.bfloat16)

    def send_block(to, source, device):
        leaving[to] = gather_block(to)
        row_copy(to, me, device).start()

    for_partners(send_block)
    arrived[me] = gather_block(me)

    def gramian(index, total):
        at = pl.ds(pl.multiple_of(index * chunk, chunk), chunk)
        block = table[at, :]
        return total + lax.dot_general(block, block, TN, preferred_element_type=f32)

    own = lax.fori_loop(
        0, table.shape[0] // chunk, gramian, jnp.zeros((features, features), f32)
    )
    for index in range(count):
        parts[index] = own[index * share:(index + 1) * share]
    for_partners(lambda to, source, device: part_copy(to, me, device).start())
    partial[me] = parts[me]

    def products(owner, vector_parts, total):
        inner = joined(
            lax.dot_general(vector_parts, arrived[owner], NT, preferred_element_type=f32)
        )
        inner = jnp.where(marks[owner] > 0.0, inner, 0.0)
        return total + jnp.dot(split(inner), scaled[owner], preferred_element_type=f32)

    start_parts = split(start_ref[...])
    image[...] = jnp.zeros_like(image)
    target[...] = jnp.zeros_like(target)
    ones = jnp.ones((users, features), jnp.bfloat16)

    def take_block(owner):
        marked = marks[owner]
        spread = lax.dot_general(
            marked.astype(jnp.bfloat16), ones, TN, preferred_element_type=f32
        )
        scaled[owner] = (spread * arrived[owner].astype(f32)).astype(jnp.bfloat16)
        member = jnp.where(marked > 0.0, 1.0, 0.0).astype(jnp.bfloat16)
        target[...] += jnp.dot(member, scaled[owner], preferred_element_type=f32)
        image[...] = products(owner, start_parts, image[...])

    def receive_block(to, source, device):
        row_copy(to, source, device).wait()
        take_block(source)

    take_block(me)
    middle = count // 2
    for_partners(receive_block, 0, middle)
    for_partners(finish(part_copy))
    summed[...] = jnp.sum(partial[...], axis=0)
    for_partners(lambda to, source, device: whole_copy(to, me, device).start())
    whole[me] = summed[...]
    for_partners(receive_block, middle)
    for_partners(finish(whole_copy))

    for index in range(count):
        shared[index * share:(index + 1) * share, :] = whole[index]
    line = lax.broadcasted_iota(jnp.int32, (features, features), 0)
    column = lax.broadcasted_iota(jnp.int32, (features, features), 1)
    shared[...] = shared[...] * (slot_count / total_items) + jnp.where(
        line == column, 0.5 * slot_count, 0.0
    )

    def common(value):
        return lax.dot_general(
            value, shared[...], NT, precision=lax.Precision.HIGHEST, preferred_element_type=f32
        )

    def apply_system(value):
        vector_parts = split(value)
        unroll = 4

        def some(index, total):
            for j in range(unroll):
                total = products(index * unroll + j, vector_parts, total)
            return total

        total = lax.fori_loop(
            0, count // unroll, some, jnp.zeros((2 * users, features), f32)
        )
        return common(value) + joined(total)

    estimate = start_ref[...]
    residual = target[...] - (common(estimate) + joined(image[...]))
    direction = residual
    norm_now = jnp.sum(residual * residual, axis=1, keepdims=True)
    for _ in range(CG_STEPS):
        moved = apply_system(direction)
        curvature = jnp.sum(direction * moved, axis=1, keepdims=True)
        step_len = norm_now / (curvature + 1e-06)
        estimate = estimate + step_len * direction
        residual = residual - step_len * moved
        norm_next = jnp.sum(residual * residual, axis=1, keepdims=True)
        direction = residual + norm_next / (norm_now + 1e-06) * direction
        norm_now = norm_next
    out_ref[...] = estimate


def per_device(item_table, user_rows, link_rows, link_slots, link_weights, link_counts):
    user_count, features = user_rows.shape
    slot_count = link_rows.shape[1]
    devices = lax.axis_size("rows") * lax.axis_size("table")
    capacity = user_count * slot_count // devices
    share = features // devices
    total_items = item_table.shape[0] * devices
    vmem = pl.BlockSpec(memory_space=pltpu.VMEM)
    smem = pl.BlockSpec(memory_space=pltpu.SMEM)
    hbm = pl.BlockSpec(memory_space=pl.ANY)
    dma = pltpu.SemaphoreType.DMA
    f32, bf16, i32 = jnp.float32, jnp.bfloat16, jnp.int32

    return pl.pallas_call(
        functools.partial(sweep_kernel, total_items),
        out_shape=jax.ShapeDtypeStruct((user_count, features), f32),
        in_specs=[smem, hbm, vmem, vmem, vmem, vmem],
        out_specs=vmem,
        scratch_shapes=[
            pltpu.VMEM(item_table.shape, bf16),
            pltpu.VMEM(item_table.shape, f32),
            pltpu.VMEM((devices, 1, capacity), i32),
            pltpu.VMEM((devices, 1, capacity), i32),
            pltpu.SMEM((devices, 1, capacity), i32),
            pltpu.VMEM((2, devices, 1, capacity), f32),
            pltpu.VMEM((devices, user_count, capacity), f32),
            pltpu.VMEM((capacity, features), f32),
            pltpu.VMEM((devices, capacity, features), bf16),
            pltpu.VMEM((devices, capacity, features), bf16),
            pltpu.VMEM((devices, capacity, features), bf16),
            pltpu.VMEM((devices, share, features), f32),
            pltpu.VMEM((devices, share, features), f32),
            pltpu.VMEM((share, features), f32),
            pltpu.VMEM((devices, share, features), f32),
            pltpu.VMEM((features, features), f32),
            pltpu.VMEM((2 * user_count, features), f32),
            pltpu.VMEM((user_count, features), f32),
            dma, dma,
            dma((2, devices)), dma((2, devices)), dma((2, devices)), dma((2, devices)),
        ],
        compiler_params=pltpu.CompilerParams(
            collective_id=0, has_side_effects=True, vmem_limit_bytes=VMEM_BYTES
        ),
        name="sweep",
    )(link_counts, item_table, link_slots, link_rows, link_weights, user_rows)


def solution(mesh):
    flat = P(("rows", "table"), None)
    return jax.shard_map(
        per_device,
        mesh=mesh,
        in_specs=(flat, flat, flat, flat, flat, P(("rows", "table"))),
        out_specs=flat,
        check_vma=False,
    )
```

```python
import functools

import jax
import jax.numpy as jnp
from jax import lax
from jax.experimental import pallas as pl
from jax.experimental.pallas import tpu as pltpu
from jax.sharding import PartitionSpec as P

CG_STEPS = 3
MESH = pl.DeviceIdType.MESH
VMEM_BYTES = 64 * 1024 * 1024 - 65536
NT = (((1,), (1,)), ((), ()))
TN = (((0,), (0,)), ((), ()))


def position():
    width = lax.axis_size("table")
    count = lax.axis_size("rows") * width
    return lax.axis_index("rows") * width + lax.axis_index("table"), count, width


def partner(step):
    me, count, width = position()
    away = (step + 1) // 2 + lax.rem(step + 1, 2) * (count // 2)
    later, earlier = lax.rem(me + away, count), lax.rem(me - away + count, count)
    return later, earlier, (later // width, lax.rem(later, width))


def for_partners(body, first=0, last=None):
    _, count, _ = position()

    def step_body(step, carry):
        body(*partner(step))
        return carry

    lax.fori_loop(first, count - 1 if last is None else last, step_body, 0)


def split(value):
    high = value.astype(jnp.bfloat16)
    low = (value - high.astype(jnp.float32)).astype(jnp.bfloat16)
    return jnp.concatenate([high, low], axis=0)


def joined(value):
    half = value.shape[0] // 2
    return value[:half] + value[half:]


def place_links(slots_ref, rows_ref, weights_ref, counts_ref, owners, capacity):
    users, width = slots_ref.shape
    shift = capacity.bit_length() - 1
    group = 8

    def one_group(index, total):
        at = pl.ds(pl.multiple_of(index * group, group), group)
        slots, rows = slots_ref[at, :], rows_ref[at, :]
        owner, inner = slots >> shift, slots & (capacity - 1)
        high, low = (rows >> 7).astype(jnp.float32), (rows & 127).astype(jnp.float32)
        line = lax.broadcasted_iota(jnp.int32, (group, width), 0)
        limit = jnp.zeros((group, width), jnp.int32)
        for j in range(group):
            limit = jnp.where(line == j, counts_ref[index * group + j], limit)
        live = lax.broadcasted_iota(jnp.int32, (group, width), 1) < limit
        confidence = jnp.where(live, 1.0 + weights_ref[at, :].astype(jnp.float32) / 8.0, 0.0)
        member = (line + index * group).astype(jnp.float32)
        for user in range(group):
            pick = slice(user, user + 1)
            match = lax.broadcasted_iota(jnp.int32, (owners, width), 0) == owner[pick]
            left = jnp.concatenate(
                [jnp.where(match, part[pick], 0.0) for part in (high, low, member, confidence)],
                axis=0,
            ).astype(jnp.bfloat16)
            hit = lax.broadcasted_iota(jnp.int32, (capacity, width), 0) == inner[pick]
            right = jnp.where(hit, 1.0, 0.0).astype(jnp.bfloat16)
            total = total + lax.dot_general(left, right, NT, preferred_element_type=jnp.float32)
        return total

    total = lax.fori_loop(
        0, users // group, one_group, jnp.zeros((4 * owners, capacity), jnp.float32)
    )
    high, low, member, confidence = (total[i * owners:(i + 1) * owners] for i in range(4))
    return (high * 128.0 + low).astype(jnp.int32), member, confidence


def gather_rows(read_index, source, target):
    group = 32

    def one_group(index, carry):
        start = index * group
        values = [source[pl.ds(read_index(start + i), 1), :] for i in range(group)]
        for i, value in enumerate(values):
            target[pl.ds(start + i, 1), :] = value
        return carry

    lax.fori_loop(0, target.shape[0] // group, one_group, 0)


def sweep_kernel(
    total_items,
    counts_hbm, table_hbm, slots_hbm, rows_hbm, weights_hbm, start_hbm, out_ref,
    counts_ref, slots_ref, rows_ref, weights_ref, start_ref, table, wide, wanted, asked, indices, placed, marks, stage, leaving, arrived, scaled,
    parts, partial, summed, whole, shared, image, target,
    input_sems, table_sem, index_sem, ask_sems, row_sems, part_sems, whole_sems,
):
    me, count, _ = position()
    users, features = start_ref.shape
    slot_count = slots_ref.shape[1]
    capacity = wanted.shape[2]
    share = features // count
    assert wide.shape[0] & (wide.shape[0] - 1) == 0
    f32 = jnp.float32

    def remote(source, landing, sems, outgoing, incoming, device):
        return pltpu.make_async_remote_copy(
            src_ref=source, dst_ref=landing,
            send_sem=sems.at[0, outgoing], recv_sem=sems.at[1, incoming],
            device_id=device, device_id_type=MESH,
        )

    def ask_copy(to, slot, device):
        return remote(wanted.at[to], asked.at[slot], ask_sems, to, slot, device)

    def row_copy(to, slot, device):
        return remote(leaving.at[to], arrived.at[slot], row_sems, to, slot, device)

    def part_copy(to, slot, device):
        return remote(parts.at[to], partial.at[slot], part_sems, to, slot, device)

    def whole_copy(to, slot, device):
        return remote(summed, whole.at[slot], whole_sems, to, slot, device)

    def finish(copy):
        def both(to, source, device):
            copy(to, source, device).wait()

        return both

    loads = [
        pltpu.make_async_copy(source, landing, input_sems.at[index])
        for index, (source, landing) in enumerate([
            (slots_hbm, slots_ref), (rows_hbm, rows_ref), (counts_hbm, counts_ref),
            (weights_hbm, weights_ref), (start_hbm, start_ref),
        ])
    ]
    for load in loads:
        load.start()
    load_table = pltpu.make_async_copy(table_hbm, table, table_sem)
    load_table.start()
    barrier = pltpu.get_barrier_semaphore()
    for_partners(
        lambda to, source, device: pl.semaphore_signal(
            barrier, inc=1, device_id=device, device_id_type=MESH
        )
    )
    for load in loads:
        load.wait()
    rows, member, confidence = place_links(
        slots_ref, rows_ref, weights_ref, counts_ref, count, capacity
    )
    wanted[...] = rows[:, None, :]
    placed[0] = member[:, None, :]
    placed[1] = confidence[:, None, :]
    pl.semaphore_wait(barrier, count - 1)
    for_partners(lambda to, source, device: ask_copy(to, me, device).start())
    asked[me] = wanted[me]

    def mark(owner, carry):
        line = lax.broadcasted_iota(jnp.int32, (users, capacity), 0)
        hit = line == placed[0, owner].astype(jnp.int32)
        marks[owner] = jnp.where(hit, placed[1, owner], 0.0)
        return carry

    lax.fori_loop(0, count, mark, 0)

    chunk = 1024
    load_table.wait()

    def widen(index, carry):
        at = pl.ds(pl.multiple_of(index * chunk, chunk), chunk)
        wide[at, :] = table[at, :].astype(f32)
        return carry

    lax.fori_loop(0, table.shape[0] // chunk, widen, 0)

    for_partners(finish(ask_copy))
    load_indices = pltpu.make_async_copy(asked, indices, index_sem)
    load_indices.start()
    load_indices.wait()

    def gather_block(owner):
        gather_rows(lambda i: indices[owner, 0, i] & (wide.shape[0] - 1), wide, stage)
        return stage[...].astype(jnp.bfloat16)

    def send_block(to, source, device):
        leaving[to] = gather_block(to)
        row_copy(to, me, device).start()

    for_partners(send_block)
    arrived[me] = gather_block(me)

    def gramian(index, total):
        at = pl.ds(pl.multiple_of(index * chunk, chunk), chunk)
        block = table[at, :]
        return total + lax.dot_general(block, block, TN, preferred_element_type=f32)

    own = lax.fori_loop(
        0, table.shape[0] // chunk, gramian, jnp.zeros((features, features), f32)
    )
    for index in range(count):
        parts[index] = own[index * share:(index + 1) * share]
    for_partners(lambda to, source, device: part_copy(to, me, device).start())
    partial[me] = parts[me]

    def products(owner, vector_parts, total):
        inner = joined(
            lax.dot_general(vector_parts, arrived[owner], NT, preferred_element_type=f32)
        )
        inner = jnp.where(marks[owner] > 0.0, inner, 0.0)
        return total + jnp.dot(split(inner), scaled[owner], preferred_element_type=f32)

    start_parts = split(start_ref[...])
    image[...] = jnp.zeros_like(image)
    target[...] = jnp.zeros_like(target)
    ones = jnp.ones((users, features), jnp.bfloat16)

    def take_block(owner):
        marked = marks[owner]
        spread = lax.dot_general(
            marked.astype(jnp.bfloat16), ones, TN, preferred_element_type=f32
        )
        scaled[owner] = (spread * arrived[owner].astype(f32)).astype(jnp.bfloat16)
        member = jnp.where(marked > 0.0, 1.0, 0.0).astype(jnp.bfloat16)
        target[...] += jnp.dot(member, scaled[owner], preferred_element_type=f32)
        image[...] = products(owner, start_parts, image[...])

    def receive_block(to, source, device):
        row_copy(to, source, device).wait()
        take_block(source)

    take_block(me)
    middle = count // 2
    for_partners(receive_block, 0, middle)
    for_partners(finish(part_copy))
    summed[...] = jnp.sum(partial[...], axis=0)
    for_partners(lambda to, source, device: whole_copy(to, me, device).start())
    whole[me] = summed[...]
    for_partners(receive_block, middle)
    for_partners(finish(whole_copy))

    for index in range(count):
        shared[index * share:(index + 1) * share, :] = whole[index]
    line = lax.broadcasted_iota(jnp.int32, (features, features), 0)
    column = lax.broadcasted_iota(jnp.int32, (features, features), 1)
    shared[...] = shared[...] * (slot_count / total_items) + jnp.where(
        line == column, 0.5 * slot_count, 0.0
    )

    def common(value):
        return lax.dot_general(
            value, shared[...], NT, precision=lax.Precision.HIGHEST, preferred_element_type=f32
        )

    def apply_system(value):
        vector_parts = split(value)
        unroll = 4

        def some(index, total):
            for j in range(unroll):
                total = products(index * unroll + j, vector_parts, total)
            return total

        total = lax.fori_loop(
            0, count // unroll, some, jnp.zeros((2 * users, features), f32)
        )
        return common(value) + joined(total)

    estimate = start_ref[...]
    residual = target[...] - (common(estimate) + joined(image[...]))
    direction = residual
    norm_now = jnp.sum(residual * residual, axis=1, keepdims=True)
    for _ in range(CG_STEPS):
        moved = apply_system(direction)
        curvature = jnp.sum(direction * moved, axis=1, keepdims=True)
        step_len = norm_now / (curvature + 1e-06)
        estimate = estimate + step_len * direction
        residual = residual - step_len * moved
        norm_next = jnp.sum(residual * residual, axis=1, keepdims=True)
        direction = residual + norm_next / (norm_now + 1e-06) * direction
        norm_now = norm_next
    out_ref[...] = estimate


def per_device(item_table, user_rows, link_rows, link_slots, link_weights, link_counts):
    user_count, features = user_rows.shape
    slot_count = link_rows.shape[1]
    devices = lax.axis_size("rows") * lax.axis_size("table")
    capacity = user_count * slot_count // devices
    share = features // devices
    total_items = item_table.shape[0] * devices
    vmem = pl.BlockSpec(memory_space=pltpu.VMEM)
    hbm = pl.BlockSpec(memory_space=pltpu.HBM)
    dma = pltpu.SemaphoreType.DMA
    f32, bf16, i32 = jnp.float32, jnp.bfloat16, jnp.int32

    return pl.pallas_call(
        functools.partial(sweep_kernel, total_items),
        out_shape=jax.ShapeDtypeStruct((user_count, features), f32),
        in_specs=[hbm] * 6,
        out_specs=vmem,
        scratch_shapes=[
            pltpu.SMEM(link_counts.shape, i32),
            pltpu.VMEM(link_slots.shape, i32),
            pltpu.VMEM(link_rows.shape, i32),
            pltpu.VMEM(link_weights.shape, i32),
            pltpu.VMEM(user_rows.shape, f32),
            pltpu.VMEM(item_table.shape, bf16),
            pltpu.VMEM(item_table.shape, f32),
            pltpu.VMEM((devices, 1, capacity), i32),
            pltpu.VMEM((devices, 1, capacity), i32),
            pltpu.SMEM((devices, 1, capacity), i32),
            pltpu.VMEM((2, devices, 1, capacity), f32),
            pltpu.VMEM((devices, user_count, capacity), f32),
            pltpu.VMEM((capacity, features), f32),
            pltpu.VMEM((devices, capacity, features), bf16),
            pltpu.VMEM((devices, capacity, features), bf16),
            pltpu.VMEM((devices, capacity, features), bf16),
            pltpu.VMEM((devices, share, features), f32),
            pltpu.VMEM((devices, share, features), f32),
            pltpu.VMEM((share, features), f32),
            pltpu.VMEM((devices, share, features), f32),
            pltpu.VMEM((features, features), f32),
            pltpu.VMEM((2 * user_count, features), f32),
            pltpu.VMEM((user_count, features), f32),
            dma((5,)), dma, dma,
            dma((2, devices)), dma((2, devices)), dma((2, devices)), dma((2, devices)),
        ],
        compiler_params=pltpu.CompilerParams(
            collective_id=0, has_side_effects=True, vmem_limit_bytes=VMEM_BYTES
        ),
        name="sweep",
    )(link_counts, item_table, link_slots, link_rows, link_weights, user_rows)


def solution(mesh):
    flat = P(("rows", "table"), None)
    return jax.shard_map(
        per_device,
        mesh=mesh,
        in_specs=(flat, flat, flat, flat, flat, P(("rows", "table"))),
        out_specs=flat,
        check_vma=False,
    )
```

```python
import functools

import jax
import jax.numpy as jnp
from jax import lax
from jax.experimental import pallas as pl
from jax.experimental.pallas import tpu as pltpu
from jax.sharding import PartitionSpec as P

CG_STEPS = 3
MESH = pl.DeviceIdType.MESH
VMEM_BYTES = 64 * 1024 * 1024 - 65536
NT = (((1,), (1,)), ((), ()))
TN = (((0,), (0,)), ((), ()))


def position():
    width = lax.axis_size("table")
    count = lax.axis_size("rows") * width
    return lax.axis_index("rows") * width + lax.axis_index("table"), count, width


def partner(step):
    me, count, width = position()
    away = (step + 1) // 2 + lax.rem(step + 1, 2) * (count // 2)
    later, earlier = lax.rem(me + away, count), lax.rem(me - away + count, count)
    return later, earlier, (later // width, lax.rem(later, width))


def for_partners(body, first=0, last=None):
    _, count, _ = position()

    def step_body(step, carry):
        body(*partner(step))
        return carry

    lax.fori_loop(first, count - 1 if last is None else last, step_body, 0)


def split(value):
    high = value.astype(jnp.bfloat16)
    low = (value - high.astype(jnp.float32)).astype(jnp.bfloat16)
    return jnp.concatenate([high, low], axis=0)


def joined(value):
    half = value.shape[0] // 2
    return value[:half] + value[half:]


def place(slots_ref, read_parts, owners, capacity):
    users, width = slots_ref.shape
    shift = capacity.bit_length() - 1
    group = 8

    def one_group(index, total):
        at = pl.ds(pl.multiple_of(index * group, group), group)
        slots = slots_ref[at, :]
        owner, inner = slots >> shift, slots & (capacity - 1)
        parts = read_parts(index * group, at)

        def choose(user):
            pick = slice(user, user + 1)
            match = lax.broadcasted_iota(jnp.int32, (owners, width), 0) == owner[pick]
            left = jnp.concatenate([jnp.where(match, part[pick], 0.0) for part in parts], axis=0)
            hit = lax.broadcasted_iota(jnp.int32, (capacity, width), 0) == inner[pick]
            return left.astype(jnp.bfloat16), jnp.where(hit, 1.0, 0.0).astype(jnp.bfloat16)

        for user in range(0, group, 2):
            lefts, rights = zip(choose(user), choose(user + 1))
            total = total + lax.dot_general(
                jnp.concatenate(lefts, axis=1), jnp.concatenate(rights, axis=1), NT,
                preferred_element_type=jnp.float32,
            )
        return total

    total = lax.fori_loop(
        0, users // group, one_group, jnp.zeros((2 * owners, capacity), jnp.float32)
    )
    return total[:owners], total[owners:]


def gather_rows(read_index, source, target):
    group = 32

    def one_group(index, carry):
        start = index * group
        values = [source[pl.ds(read_index(start + i), 1), :] for i in range(group)]
        for i, value in enumerate(values):
            target[pl.ds(start + i, 1), :] = value
        return carry

    lax.fori_loop(0, target.shape[0] // group, one_group, 0)


def sweep_kernel(
    total_items,
    counts_hbm, table_hbm, slots_hbm, rows_hbm, weights_hbm, start_hbm, out_ref,
    counts_ref, slots_ref, rows_ref, weights_ref, start_ref, table, wide, wanted, asked, indices, placed, marks, stage, leaving, arrived, scaled,
    parts, partial, summed, whole, shared, image, target,
    input_sems, table_sem, index_sem, ask_sems, row_sems, part_sems, whole_sems,
):
    me, count, _ = position()
    users, features = start_ref.shape
    slot_count = slots_ref.shape[1]
    capacity = wanted.shape[2]
    share = features // count
    assert wide.shape[0] & (wide.shape[0] - 1) == 0
    f32 = jnp.float32

    def remote(source, landing, sems, outgoing, incoming, device):
        return pltpu.make_async_remote_copy(
            src_ref=source, dst_ref=landing,
            send_sem=sems.at[0, outgoing], recv_sem=sems.at[1, incoming],
            device_id=device, device_id_type=MESH,
        )

    def ask_copy(to, slot, device):
        return remote(wanted.at[to], asked.at[slot], ask_sems, to, slot, device)

    def row_copy(to, slot, device):
        return remote(leaving.at[to], arrived.at[slot], row_sems, to, slot, device)

    def part_copy(to, slot, device):
        return remote(parts.at[to], partial.at[slot], part_sems, to, slot, device)

    def whole_copy(to, slot, device):
        return remote(summed, whole.at[slot], whole_sems, to, slot, device)

    def finish(copy):
        def both(to, source, device):
            copy(to, source, device).wait()

        return both

    loads = [
        pltpu.make_async_copy(source, landing, input_sems.at[index])
        for index, (source, landing) in enumerate([
            (slots_hbm, slots_ref), (rows_hbm, rows_ref), (counts_hbm, counts_ref),
            (weights_hbm, weights_ref), (start_hbm, start_ref),
        ])
    ]
    for load in loads:
        load.start()
    load_table = pltpu.make_async_copy(table_hbm, table, table_sem)
    load_table.start()
    barrier = pltpu.get_barrier_semaphore()
    for_partners(
        lambda to, source, device: pl.semaphore_signal(
            barrier, inc=1, device_id=device, device_id_type=MESH
        )
    )
    for load in loads[:2]:
        load.wait()

    def row_parts(first, at):
        rows = rows_ref[at, :]
        return (rows >> 7).astype(f32), (rows & 127).astype(f32)

    high, low = place(slots_ref, row_parts, count, capacity)
    wanted[...] = (high * 128.0 + low).astype(jnp.int32)[:, None, :]
    pl.semaphore_wait(barrier, count - 1)
    for_partners(lambda to, source, device: ask_copy(to, me, device).start())
    asked[me] = wanted[me]

    chunk = 1024
    load_table.wait()

    def widen(index, carry):
        at = pl.ds(pl.multiple_of(index * chunk, chunk), chunk)
        wide[at, :] = table[at, :].astype(f32)
        return carry

    lax.fori_loop(0, table.shape[0] // chunk, widen, 0)

    for_partners(finish(ask_copy))
    load_indices = pltpu.make_async_copy(asked, indices, index_sem)
    load_indices.start()
    load_indices.wait()

    def gather_block(owner):
        gather_rows(lambda i: indices[owner, 0, i] & (wide.shape[0] - 1), wide, stage)
        return stage[...].astype(jnp.bfloat16)

    def send_block(to, source, device):
        leaving[to] = gather_block(to)
        row_copy(to, me, device).start()

    for_partners(send_block)
    arrived[me] = gather_block(me)

    for load in loads[2:]:
        load.wait()

    def link_parts(first, at):
        shape = (8, slot_count)
        line = lax.broadcasted_iota(jnp.int32, shape, 0)
        limit = jnp.zeros(shape, jnp.int32)
        for j in range(shape[0]):
            limit = jnp.where(line == j, counts_ref[first + j], limit)
        live = lax.broadcasted_iota(jnp.int32, shape, 1) < limit
        confidence = jnp.where(live, 1.0 + weights_ref[at, :].astype(f32) / 8.0, 0.0)
        return (line + first).astype(f32), confidence

    member, confidence = place(slots_ref, link_parts, count, capacity)
    placed[0] = member[:, None, :]
    placed[1] = confidence[:, None, :]

    def mark(owner, carry):
        line = lax.broadcasted_iota(jnp.int32, (users, capacity), 0)
        hit = line == placed[0, owner].astype(jnp.int32)
        marks[owner] = jnp.where(hit, placed[1, owner], 0.0)
        return carry

    lax.fori_loop(0, count, mark, 0)

    def gramian(index, total):
        at = pl.ds(pl.multiple_of(index * chunk, chunk), chunk)
        block = table[at, :]
        return total + lax.dot_general(block, block, TN, preferred_element_type=f32)

    own = lax.fori_loop(
        0, table.shape[0] // chunk, gramian, jnp.zeros((features, features), f32)
    )
    for index in range(count):
        parts[index] = own[index * share:(index + 1) * share]
    for_partners(lambda to, source, device: part_copy(to, me, device).start())
    partial[me] = parts[me]

    def products(owner, vector_parts, total, weighted):
        inner = joined(
            lax.dot_general(vector_parts, arrived[owner], NT, preferred_element_type=f32)
        )
        inner = jnp.where(marks[owner] > 0.0, inner, 0.0)
        return total + jnp.dot(split(inner), weighted, preferred_element_type=f32)

    start_parts = split(start_ref[...])
    image[...] = jnp.zeros_like(image)
    target[...] = jnp.zeros_like(target)
    ones = jnp.ones((users, features), jnp.bfloat16)

    def take_blocks(owners):
        goals, images = target[...], image[...]
        for owner in owners:
            marked = marks[owner]
            spread = lax.dot_general(
                marked.astype(jnp.bfloat16), ones, TN, preferred_element_type=f32
            )
            weighted = (spread * arrived[owner].astype(f32)).astype(jnp.bfloat16)
            scaled[owner] = weighted
            member = jnp.where(marked > 0.0, 1.0, 0.0).astype(jnp.bfloat16)
            goals = goals + jnp.dot(member, weighted, preferred_element_type=f32)
            images = products(owner, start_parts, images, weighted)
        target[...] = goals
        image[...] = images

    def receive_blocks(steps):
        sources = []
        for step in steps:
            to, source, device = partner(step)
            row_copy(to, source, device).wait()
            sources.append(source)
        take_blocks(sources)

    def receive_pair(index, carry):
        receive_blocks([2 * index + 1, 2 * index + 2])
        return carry

    take_blocks([me])
    receive_blocks([0])
    pairs = (count - 2) // 2
    lax.fori_loop(0, pairs // 2, receive_pair, 0)
    for_partners(finish(part_copy))
    summed[...] = jnp.sum(partial[...], axis=0)
    for_partners(lambda to, source, device: whole_copy(to, me, device).start())
    whole[me] = summed[...]
    lax.fori_loop(pairs // 2, pairs, receive_pair, 0)
    for_partners(finish(whole_copy))

    for index in range(count):
        shared[index * share:(index + 1) * share, :] = whole[index]
    line = lax.broadcasted_iota(jnp.int32, (features, features), 0)
    column = lax.broadcasted_iota(jnp.int32, (features, features), 1)
    shared[...] = shared[...] * (slot_count / total_items) + jnp.where(
        line == column, 0.5 * slot_count, 0.0
    )

    def common(value):
        return lax.dot_general(
            value, shared[...], NT, precision=lax.Precision.HIGHEST, preferred_element_type=f32
        )

    def apply_system(value):
        vector_parts = split(value)
        unroll = 8

        def some(index, total):
            for j in range(unroll):
                owner = index * unroll + j
                total = products(owner, vector_parts, total, scaled[owner])
            return total

        total = lax.fori_loop(
            0, count // unroll, some, jnp.zeros((2 * users, features), f32)
        )
        return common(value) + joined(total)

    estimate = start_ref[...]
    residual = target[...] - (common(estimate) + joined(image[...]))
    direction = residual
    norm_now = jnp.sum(residual * residual, axis=1, keepdims=True)
    for _ in range(CG_STEPS):
        moved = apply_system(direction)
        curvature = jnp.sum(direction * moved, axis=1, keepdims=True)
        step_len = norm_now / (curvature + 1e-06)
        estimate = estimate + step_len * direction
        residual = residual - step_len * moved
        norm_next = jnp.sum(residual * residual, axis=1, keepdims=True)
        direction = residual + norm_next / (norm_now + 1e-06) * direction
        norm_now = norm_next
    out_ref[...] = estimate


def per_device(item_table, user_rows, link_rows, link_slots, link_weights, link_counts):
    user_count, features = user_rows.shape
    slot_count = link_rows.shape[1]
    devices = lax.axis_size("rows") * lax.axis_size("table")
    capacity = user_count * slot_count // devices
    share = features // devices
    total_items = item_table.shape[0] * devices
    vmem = pl.BlockSpec(memory_space=pltpu.VMEM)
    hbm = pl.BlockSpec(memory_space=pltpu.HBM)
    dma = pltpu.SemaphoreType.DMA
    f32, bf16, i32 = jnp.float32, jnp.bfloat16, jnp.int32

    return pl.pallas_call(
        functools.partial(sweep_kernel, total_items),
        out_shape=jax.ShapeDtypeStruct((user_count, features), f32),
        in_specs=[hbm] * 6,
        out_specs=vmem,
        scratch_shapes=[
            pltpu.SMEM(link_counts.shape, i32),
            pltpu.VMEM(link_slots.shape, i32),
            pltpu.VMEM(link_rows.shape, i32),
            pltpu.VMEM(link_weights.shape, i32),
            pltpu.VMEM(user_rows.shape, f32),
            pltpu.VMEM(item_table.shape, bf16),
            pltpu.VMEM(item_table.shape, f32),
            pltpu.VMEM((devices, 1, capacity), i32),
            pltpu.VMEM((devices, 1, capacity), i32),
            pltpu.SMEM((devices, 1, capacity), i32),
            pltpu.VMEM((2, devices, 1, capacity), f32),
            pltpu.VMEM((devices, user_count, capacity), f32),
            pltpu.VMEM((capacity, features), f32),
            pltpu.VMEM((devices, capacity, features), bf16),
            pltpu.VMEM((devices, capacity, features), bf16),
            pltpu.VMEM((devices, capacity, features), bf16),
            pltpu.VMEM((devices, share, features), f32),
            pltpu.VMEM((devices, share, features), f32),
            pltpu.VMEM((share, features), f32),
            pltpu.VMEM((devices, share, features), f32),
            pltpu.VMEM((features, features), f32),
            pltpu.VMEM((2 * user_count, features), f32),
            pltpu.VMEM((user_count, features), f32),
            dma((5,)), dma, dma,
            dma((2, devices)), dma((2, devices)), dma((2, devices)), dma((2, devices)),
        ],
        compiler_params=pltpu.CompilerParams(
            collective_id=0, has_side_effects=True, vmem_limit_bytes=VMEM_BYTES
        ),
        name="sweep",
    )(link_counts, item_table, link_slots, link_rows, link_weights, user_rows)


def solution(mesh):
    flat = P(("rows", "table"), None)
    return jax.shard_map(
        per_device,
        mesh=mesh,
        in_specs=(flat, flat, flat, flat, flat, P(("rows", "table"))),
        out_specs=flat,
        check_vma=False,
    )
```

```python
import functools

import jax
import jax.numpy as jnp
from jax import lax
from jax.experimental import pallas as pl
from jax.experimental.pallas import tpu as pltpu
from jax.sharding import PartitionSpec as P

CG_STEPS = 3
MESH = pl.DeviceIdType.MESH
VMEM_BYTES = 64 * 1024 * 1024 - 65536
NT = (((1,), (1,)), ((), ()))
TN = (((0,), (0,)), ((), ()))


def position():
    width = lax.axis_size("table")
    count = lax.axis_size("rows") * width
    return lax.axis_index("rows") * width + lax.axis_index("table"), count, width


def partner(step):
    me, count, width = position()
    away = lax.div(step + 1, 2) + lax.rem(step + 1, 2) * (count // 2)
    later, earlier = me + away, me - away
    later = jnp.where(later >= count, later - count, later)
    earlier = jnp.where(earlier < 0, earlier + count, earlier)
    return later, earlier, (lax.div(later, width), lax.rem(later, width))


def for_partners(body, first=0, last=None):
    _, count, _ = position()

    def step_body(step, carry):
        body(*partner(step))
        return carry

    lax.fori_loop(first, count - 1 if last is None else last, step_body, 0)


def split(value):
    high = value.astype(jnp.bfloat16)
    low = (value - high.astype(jnp.float32)).astype(jnp.bfloat16)
    return jnp.concatenate([high, low], axis=0)


def joined(value):
    half = value.shape[0] // 2
    return value[:half] + value[half:]


def place(slots_ref, read_parts, owners, capacity):
    users, width = slots_ref.shape
    shift = capacity.bit_length() - 1
    group = 8

    def one_group(index, total):
        at = pl.ds(pl.multiple_of(index * group, group), group)
        slots = slots_ref[at, :]
        owner, inner = slots >> shift, slots & (capacity - 1)
        parts = read_parts(index * group, at)

        def choose(user):
            pick = slice(user, user + 1)
            match = lax.broadcasted_iota(jnp.int32, (owners, width), 0) == owner[pick]
            left = jnp.concatenate([jnp.where(match, part[pick], 0.0) for part in parts], axis=0)
            hit = lax.broadcasted_iota(jnp.int32, (capacity, width), 0) == inner[pick]
            return left.astype(jnp.bfloat16), jnp.where(hit, 1.0, 0.0).astype(jnp.bfloat16)

        for user in range(0, group, 2):
            lefts, rights = zip(choose(user), choose(user + 1))
            total = total + lax.dot_general(
                jnp.concatenate(lefts, axis=1), jnp.concatenate(rights, axis=1), NT,
                preferred_element_type=jnp.float32,
            )
        return total

    total = lax.fori_loop(
        0, users // group, one_group, jnp.zeros((2 * owners, capacity), jnp.float32)
    )
    return total[:owners], total[owners:]


def gather_rows(read_index, source, target):
    group = 32

    def one_group(index, carry):
        start = index * group
        values = [source[pl.ds(read_index(start + i), 1), :] for i in range(group)]
        for i, value in enumerate(values):
            target[pl.ds(start + i, 1), :] = value
        return carry

    lax.fori_loop(0, target.shape[0] // group, one_group, 0)


def sweep_kernel(
    total_items,
    counts_hbm, table_hbm, slots_hbm, rows_hbm, weights_hbm, start_hbm, out_ref,
    counts_ref, slots_ref, rows_ref, weights_ref, start_ref, table, wide, wanted, asked, indices, placed, marks, stage, leaving, arrived, scaled,
    parts, partial, summed, whole, shared, image, target,
    input_sems, table_sem, index_sem, ask_sems, row_sems, part_sems, whole_sems,
):
    me, count, _ = position()
    users, features = start_ref.shape
    slot_count = slots_ref.shape[1]
    capacity = wanted.shape[2]
    share = features // count
    assert wide.shape[0] & (wide.shape[0] - 1) == 0
    f32 = jnp.float32

    def remote(source, landing, sems, outgoing, incoming, device):
        return pltpu.make_async_remote_copy(
            src_ref=source, dst_ref=landing,
            send_sem=sems.at[0, outgoing], recv_sem=sems.at[1, incoming],
            device_id=device, device_id_type=MESH,
        )

    def ask_copy(to, slot, device):
        return remote(wanted.at[to], asked.at[slot], ask_sems, to, slot, device)

    def row_copy(to, slot, device):
        return remote(leaving.at[to], arrived.at[slot], row_sems, to, slot, device)

    def part_copy(to, slot, device):
        return remote(parts.at[to], partial.at[slot], part_sems, to, slot, device)

    def whole_copy(to, slot, device):
        return remote(summed, whole.at[slot], whole_sems, to, slot, device)

    def finish(copy):
        def both(to, source, device):
            copy(to, source, device).wait()

        return both

    loads = [
        pltpu.make_async_copy(source, landing, input_sems.at[index])
        for index, (source, landing) in enumerate([
            (slots_hbm, slots_ref), (rows_hbm, rows_ref), (counts_hbm, counts_ref),
            (weights_hbm, weights_ref), (start_hbm, start_ref),
        ])
    ]
    for load in loads:
        load.start()
    load_table = pltpu.make_async_copy(table_hbm, table, table_sem)
    load_table.start()
    barrier = pltpu.get_barrier_semaphore()
    for_partners(
        lambda to, source, device: pl.semaphore_signal(
            barrier, inc=1, device_id=device, device_id_type=MESH
        )
    )
    for load in loads[:2]:
        load.wait()

    def row_parts(first, at):
        rows = rows_ref[at, :]
        return (rows >> 7).astype(f32), (rows & 127).astype(f32)

    high, low = place(slots_ref, row_parts, count, capacity)
    wanted[...] = (high * 128.0 + low).astype(jnp.int32)[:, None, :]
    pl.semaphore_wait(barrier, count - 1)
    for_partners(lambda to, source, device: ask_copy(to, me, device).start())
    asked[me] = wanted[me]

    chunk = 1024
    load_table.wait()

    def widen(index, carry):
        at = pl.ds(pl.multiple_of(index * chunk, chunk), chunk)
        wide[at, :] = table[at, :].astype(f32)
        return carry

    lax.fori_loop(0, table.shape[0] // chunk, widen, 0)

    for_partners(finish(ask_copy))
    load_indices = pltpu.make_async_copy(asked, indices, index_sem)
    load_indices.start()
    load_indices.wait()

    def gather_block(owner):
        gather_rows(lambda i: indices[owner, 0, i] & (wide.shape[0] - 1), wide, stage)
        return stage[...].astype(jnp.bfloat16)

    def send_block(to, source, device):
        leaving[to] = gather_block(to)
        row_copy(to, me, device).start()

    for_partners(send_block)
    arrived[me] = gather_block(me)

    for load in loads[2:]:
        load.wait()

    def link_parts(first, at):
        shape = (8, slot_count)
        line = lax.broadcasted_iota(jnp.int32, shape, 0)
        limit = jnp.zeros(shape, jnp.int32)
        for j in range(shape[0]):
            limit = jnp.where(line == j, counts_ref[first + j], limit)
        live = lax.broadcasted_iota(jnp.int32, shape, 1) < limit
        confidence = jnp.where(live, 1.0 + weights_ref[at, :].astype(f32) / 8.0, 0.0)
        return (line + first).astype(f32), confidence

    member, confidence = place(slots_ref, link_parts, count, capacity)
    placed[0] = member[:, None, :]
    placed[1] = confidence[:, None, :]

    def mark(owner, carry):
        line = lax.broadcasted_iota(jnp.int32, (users, capacity), 0)
        hit = line == placed[0, owner].astype(jnp.int32)
        marks[owner] = jnp.where(hit, placed[1, owner], 0.0)
        return carry

    lax.fori_loop(0, count, mark, 0)

    def gramian(index, total):
        at = pl.ds(pl.multiple_of(index * chunk, chunk), chunk)
        block = table[at, :]
        return total + lax.dot_general(block, block, TN, preferred_element_type=f32)

    own = lax.fori_loop(
        0, table.shape[0] // chunk, gramian, jnp.zeros((features, features), f32)
    )
    for index in range(count):
        parts[index] = own[index * share:(index + 1) * share]
    for_partners(lambda to, source, device: part_copy(to, me, device).start())
    partial[me] = parts[me]

    def products(owner, vector_parts, total, weighted):
        inner = lax.dot_general(vector_parts, arrived[owner], NT, preferred_element_type=f32)
        whole_parts = vector_parts.shape[0] == users
        inner = jnp.where(marks[owner] > 0.0, inner if whole_parts else joined(inner), 0.0)
        inner_parts = inner.astype(jnp.bfloat16) if whole_parts else split(inner)
        return total + jnp.dot(inner_parts, weighted, preferred_element_type=f32)

    start_parts = split(start_ref[...])
    image[...] = jnp.zeros_like(image)
    target[...] = jnp.zeros_like(target)
    ones = jnp.ones((users, features), jnp.bfloat16)

    def take_blocks(owners):
        goals, images = target[...], image[...]
        for owner in owners:
            marked = marks[owner]
            spread = lax.dot_general(
                marked.astype(jnp.bfloat16), ones, TN, preferred_element_type=f32
            )
            weighted = (spread * arrived[owner].astype(f32)).astype(jnp.bfloat16)
            scaled[owner] = weighted
            member = jnp.where(marked > 0.0, 1.0, 0.0).astype(jnp.bfloat16)
            goals = goals + jnp.dot(member, weighted, preferred_element_type=f32)
            images = products(owner, start_parts, images, weighted)
        target[...] = goals
        image[...] = images

    def receive_blocks(steps):
        sources = []
        for step in steps:
            to, source, device = partner(step)
            row_copy(to, source, device).wait()
            sources.append(source)
        take_blocks(sources)

    def receive_pair(index, carry):
        receive_blocks([2 * index + 1, 2 * index + 2])
        return carry

    take_blocks([me])
    receive_blocks([0])
    pairs = (count - 2) // 2
    lax.fori_loop(0, pairs // 2, receive_pair, 0)
    for_partners(finish(part_copy))
    summed[...] = jnp.sum(partial[...], axis=0)
    for_partners(lambda to, source, device: whole_copy(to, me, device).start())
    whole[me] = summed[...]
    lax.fori_loop(pairs // 2, pairs, receive_pair, 0)
    for_partners(finish(whole_copy))

    for index in range(count):
        shared[index * share:(index + 1) * share, :] = whole[index]
    line = lax.broadcasted_iota(jnp.int32, (features, features), 0)
    column = lax.broadcasted_iota(jnp.int32, (features, features), 1)
    shared[...] = shared[...] * (slot_count / total_items) + jnp.where(
        line == column, 0.5 * slot_count, 0.0
    )

    def common(value):
        return lax.dot_general(
            value, shared[...], NT, precision=lax.Precision.HIGHEST, preferred_element_type=f32
        )

    def apply_system(vector_parts):
        unroll = min(count, 32)

        def some(index, total):
            for j in range(unroll):
                owner = index * unroll + j
                total = products(owner, vector_parts, total, scaled[owner])
            return total

        nothing = jnp.zeros((vector_parts.shape[0], features), f32)
        if unroll == count:
            return some(0, nothing)
        return lax.fori_loop(0, count // unroll, some, nothing)

    estimate = start_ref[...]
    residual = target[...] - (common(estimate) + joined(image[...]))
    direction = residual
    norm_now = jnp.sum(residual * residual, axis=1, keepdims=True)
    for step in range(CG_STEPS):
        if step < CG_STEPS - 1:
            moved = common(direction) + joined(apply_system(split(direction)))
        else:
            moved = common(direction) + apply_system(direction.astype(jnp.bfloat16))
        curvature = jnp.sum(direction * moved, axis=1, keepdims=True)
        step_len = norm_now / (curvature + 1e-06)
        estimate = estimate + step_len * direction
        residual = residual - step_len * moved
        norm_next = jnp.sum(residual * residual, axis=1, keepdims=True)
        direction = residual + norm_next / (norm_now + 1e-06) * direction
        norm_now = norm_next
    out_ref[...] = estimate


def per_device(item_table, user_rows, link_rows, link_slots, link_weights, link_counts):
    user_count, features = user_rows.shape
    slot_count = link_rows.shape[1]
    devices = lax.axis_size("rows") * lax.axis_size("table")
    capacity = user_count * slot_count // devices
    share = features // devices
    total_items = item_table.shape[0] * devices
    vmem = pl.BlockSpec(memory_space=pltpu.VMEM)
    hbm = pl.BlockSpec(memory_space=pltpu.HBM)
    dma = pltpu.SemaphoreType.DMA
    f32, bf16, i32 = jnp.float32, jnp.bfloat16, jnp.int32

    return pl.pallas_call(
        functools.partial(sweep_kernel, total_items),
        out_shape=jax.ShapeDtypeStruct((user_count, features), f32),
        in_specs=[hbm] * 6,
        out_specs=vmem,
        scratch_shapes=[
            pltpu.SMEM(link_counts.shape, i32),
            pltpu.VMEM(link_slots.shape, i32),
            pltpu.VMEM(link_rows.shape, i32),
            pltpu.VMEM(link_weights.shape, i32),
            pltpu.VMEM(user_rows.shape, f32),
            pltpu.VMEM(item_table.shape, bf16),
            pltpu.VMEM(item_table.shape, f32),
            pltpu.VMEM((devices, 1, capacity), i32),
            pltpu.VMEM((devices, 1, capacity), i32),
            pltpu.SMEM((devices, 1, capacity), i32),
            pltpu.VMEM((2, devices, 1, capacity), f32),
            pltpu.VMEM((devices, user_count, capacity), f32),
            pltpu.VMEM((capacity, features), f32),
            pltpu.VMEM((devices, capacity, features), bf16),
            pltpu.VMEM((devices, capacity, features), bf16),
            pltpu.VMEM((devices, capacity, features), bf16),
            pltpu.VMEM((devices, share, features), f32),
            pltpu.VMEM((devices, share, features), f32),
            pltpu.VMEM((share, features), f32),
            pltpu.VMEM((devices, share, features), f32),
            pltpu.VMEM((features, features), f32),
            pltpu.VMEM((2 * user_count, features), f32),
            pltpu.VMEM((user_count, features), f32),
            dma((5,)), dma, dma,
            dma((2, devices)), dma((2, devices)), dma((2, devices)), dma((2, devices)),
        ],
        compiler_params=pltpu.CompilerParams(
            collective_id=0, has_side_effects=True, vmem_limit_bytes=VMEM_BYTES
        ),
        name="sweep",
    )(link_counts, item_table, link_slots, link_rows, link_weights, user_rows)


def solution(mesh):
    flat = P(("rows", "table"), None)
    return jax.shard_map(
        per_device,
        mesh=mesh,
        in_specs=(flat, flat, flat, flat, flat, P(("rows", "table"))),
        out_specs=flat,
        check_vma=False,
    )
```

```python
import functools

import jax
import jax.numpy as jnp
from jax import lax
from jax.experimental import pallas as pl
from jax.experimental.pallas import tpu as pltpu
from jax.sharding import PartitionSpec as P

CG_STEPS = 3
MESH = pl.DeviceIdType.MESH
VMEM_BYTES = 64 * 1024 * 1024 - 65536
NT = (((1,), (1,)), ((), ()))
TN = (((0,), (0,)), ((), ()))


def position():
    width = lax.axis_size("table")
    count = lax.axis_size("rows") * width
    return lax.axis_index("rows") * width + lax.axis_index("table"), count, width


def partner(step):
    me, count, width = position()
    away = lax.div(step + 1, 2) + lax.rem(step + 1, 2) * (count // 2)
    later, earlier = me + away, me - away
    later = jnp.where(later >= count, later - count, later)
    earlier = jnp.where(earlier < 0, earlier + count, earlier)
    return later, earlier, (lax.div(later, width), lax.rem(later, width))


def for_partners(body, first=0, last=None):
    _, count, _ = position()

    def step_body(step, carry):
        body(*partner(step))
        return carry

    lax.fori_loop(first, count - 1 if last is None else last, step_body, 0)


def split(value):
    high = value.astype(jnp.bfloat16)
    low = (value - high.astype(jnp.float32)).astype(jnp.bfloat16)
    return jnp.concatenate([high, low], axis=0)


def joined(value):
    half = value.shape[0] // 2
    return value[:half] + value[half:]


def place(slots_ref, read_parts, owners, capacity):
    users, width = slots_ref.shape
    shift = capacity.bit_length() - 1
    group = 8

    def one_group(index, total):
        at = pl.ds(pl.multiple_of(index * group, group), group)
        slots = slots_ref[at, :]
        owner, inner = slots >> shift, slots & (capacity - 1)
        parts = read_parts(index * group, at)

        def choose(user):
            pick = slice(user, user + 1)
            match = lax.broadcasted_iota(jnp.int32, (owners, width), 0) == owner[pick]
            left = jnp.concatenate([jnp.where(match, part[pick], 0.0) for part in parts], axis=0)
            hit = lax.broadcasted_iota(jnp.int32, (capacity, width), 0) == inner[pick]
            return left.astype(jnp.bfloat16), jnp.where(hit, 1.0, 0.0).astype(jnp.bfloat16)

        for user in range(0, group, 2):
            lefts, rights = zip(choose(user), choose(user + 1))
            total = total + lax.dot_general(
                jnp.concatenate(lefts, axis=1), jnp.concatenate(rights, axis=1), NT,
                preferred_element_type=jnp.float32,
            )
        return total

    total = lax.fori_loop(
        0, users // group, one_group, jnp.zeros((2 * owners, capacity), jnp.float32)
    )
    return total[:owners], total[owners:]


def gather_rows(read_index, source, target):
    group = 32

    def one_group(index, carry):
        start = index * group
        values = [source[pl.ds(read_index(start + i), 1), :] for i in range(group)]
        for i, value in enumerate(values):
            target[pl.ds(start + i, 1), :] = value
        return carry

    lax.fori_loop(0, target.shape[0] // group, one_group, 0)


def sweep_kernel(
    total_items,
    counts_hbm, table_hbm, slots_hbm, rows_hbm, weights_hbm, start_hbm, out_ref,
    counts_ref, slots_ref, rows_ref, weights_ref, start_ref, table, wide, wanted, asked, indices, placed, marks, stage, leaving, arrived, scaled,
    parts, partial, summed, whole, shared, image, target,
    input_sems, table_sem, index_sem, ask_sems, row_sems, part_sems, whole_sems,
):
    me, count, _ = position()
    users, features = start_ref.shape
    slot_count = slots_ref.shape[1]
    capacity = wanted.shape[2]
    share = features // count
    assert wide.shape[0] & (wide.shape[0] - 1) == 0
    f32 = jnp.float32

    def remote(source, landing, sems, outgoing, incoming, device):
        return pltpu.make_async_remote_copy(
            src_ref=source, dst_ref=landing,
            send_sem=sems.at[0, outgoing], recv_sem=sems.at[1, incoming],
            device_id=device, device_id_type=MESH,
        )

    def ask_copy(to, slot, device):
        return remote(wanted.at[to], asked.at[slot], ask_sems, to, slot, device)

    def row_copy(to, slot, device):
        return remote(leaving.at[to], arrived.at[slot], row_sems, to, slot, device)

    def part_copy(to, slot, device):
        return remote(parts.at[to], partial.at[slot], part_sems, to, slot, device)

    def whole_copy(to, slot, device):
        return remote(summed, whole.at[slot], whole_sems, to, slot, device)

    def finish(copy):
        def both(to, source, device):
            copy(to, source, device).wait()

        return both

    loads = [
        pltpu.make_async_copy(source, landing, input_sems.at[index])
        for index, (source, landing) in enumerate([
            (slots_hbm, slots_ref), (rows_hbm, rows_ref), (counts_hbm, counts_ref),
            (weights_hbm, weights_ref), (start_hbm, start_ref),
        ])
    ]
    for load in loads:
        load.start()
    load_table = pltpu.make_async_copy(table_hbm, table, table_sem)
    load_table.start()
    barrier = pltpu.get_barrier_semaphore()
    for_partners(
        lambda to, source, device: pl.semaphore_signal(
            barrier, inc=1, device_id=device, device_id_type=MESH
        )
    )
    for load in loads[:2]:
        load.wait()

    def row_parts(first, at):
        rows = rows_ref[at, :]
        return (rows >> 7).astype(f32), (rows & 127).astype(f32)

    high, low = place(slots_ref, row_parts, count, capacity)
    wanted[...] = (high * 128.0 + low).astype(jnp.int32)[:, None, :]
    pl.semaphore_wait(barrier, count - 1)
    for_partners(lambda to, source, device: ask_copy(to, me, device).start())
    asked[me] = wanted[me]

    chunk = 1024
    load_table.wait()

    def widen(index, carry):
        at = pl.ds(pl.multiple_of(index * chunk, chunk), chunk)
        wide[at, :] = table[at, :].astype(f32)
        return carry

    lax.fori_loop(0, table.shape[0] // chunk, widen, 0)

    def gather_block(owner):
        gather_rows(lambda i: indices[owner, 0, i] & (wide.shape[0] - 1), wide, stage)
        return stage[...].astype(jnp.bfloat16)

    def index_copy(owner):
        return pltpu.make_async_copy(asked.at[owner], indices.at[owner], index_sem.at[owner])

    def fetch_request(step):
        to, _, device = partner(step)
        ask_copy(to, to, device).wait()
        index_copy(to).start()

    def send_block(step):
        to, _, device = partner(step)
        index_copy(to).wait()
        leaving[to] = gather_block(to)
        row_copy(to, me, device).start()

    def send_ahead(step, carry):
        fetch_request(step + 1)
        send_block(step)
        return carry

    index_copy(me).start()
    fetch_request(0)
    lax.fori_loop(0, count - 2, send_ahead, 0)
    send_block(count - 2)
    index_copy(me).wait()
    arrived[me] = gather_block(me)

    for load in loads[2:]:
        load.wait()

    def link_parts(first, at):
        shape = (8, slot_count)
        line = lax.broadcasted_iota(jnp.int32, shape, 0)
        limit = jnp.zeros(shape, jnp.int32)
        for j in range(shape[0]):
            limit = jnp.where(line == j, counts_ref[first + j], limit)
        live = lax.broadcasted_iota(jnp.int32, shape, 1) < limit
        confidence = jnp.where(live, 1.0 + weights_ref[at, :].astype(f32) / 8.0, 0.0)
        return (line + first).astype(f32), confidence

    member, confidence = place(slots_ref, link_parts, count, capacity)
    placed[0] = member[:, None, :]
    placed[1] = confidence[:, None, :]

    def mark(owner, carry):
        line = lax.broadcasted_iota(jnp.int32, (users, capacity), 0)
        hit = line == placed[0, owner].astype(jnp.int32)
        marks[owner] = jnp.where(hit, placed[1, owner], 0.0)
        return carry

    lax.fori_loop(0, count, mark, 0)

    def gramian(index, total):
        at = pl.ds(pl.multiple_of(index * chunk, chunk), chunk)
        block = table[at, :]
        return total + lax.dot_general(block, block, TN, preferred_element_type=f32)

    own = lax.fori_loop(
        0, table.shape[0] // chunk, gramian, jnp.zeros((features, features), f32)
    )
    for index in range(count):
        parts[index] = own[index * share:(index + 1) * share]
    for_partners(lambda to, source, device: part_copy(to, me, device).start())
    partial[me] = parts[me]

    def products(owner, vector_parts, total, weighted):
        inner = lax.dot_general(vector_parts, arrived[owner], NT, preferred_element_type=f32)
        whole_parts = vector_parts.shape[0] == users
        inner = jnp.where(marks[owner] > 0.0, inner if whole_parts else joined(inner), 0.0)
        inner_parts = inner.astype(jnp.bfloat16) if whole_parts else split(inner)
        return total + jnp.dot(inner_parts, weighted, preferred_element_type=f32)

    start_parts = split(start_ref[...])
    image[...] = jnp.zeros_like(image)
    target[...] = jnp.zeros_like(target)
    ones = jnp.ones((users, features), jnp.bfloat16)

    def take_blocks(owners):
        goals, images = target[...], image[...]
        for owner in owners:
            marked = marks[owner]
            spread = lax.dot_general(
                marked.astype(jnp.bfloat16), ones, TN, preferred_element_type=f32
            )
            weighted = (spread * arrived[owner].astype(f32)).astype(jnp.bfloat16)
            scaled[owner] = weighted
            member = jnp.where(marked > 0.0, 1.0, 0.0).astype(jnp.bfloat16)
            goals = goals + jnp.dot(member, weighted, preferred_element_type=f32)
            images = products(owner, start_parts, images, weighted)
        target[...] = goals
        image[...] = images

    def receive_blocks(steps):
        sources = []
        for step in steps:
            to, source, device = partner(step)
            row_copy(to, source, device).wait()
            sources.append(source)
        take_blocks(sources)

    def receive_pair(index, carry):
        receive_blocks([2 * index + 1, 2 * index + 2])
        return carry

    take_blocks([me])
    receive_blocks([0])
    pairs = (count - 2) // 2
    lax.fori_loop(0, pairs // 2, receive_pair, 0)
    for_partners(finish(part_copy))
    summed[...] = jnp.sum(partial[...], axis=0)
    for_partners(lambda to, source, device: whole_copy(to, me, device).start())
    whole[me] = summed[...]
    lax.fori_loop(pairs // 2, pairs, receive_pair, 0)
    for_partners(finish(whole_copy))

    for index in range(count):
        shared[index * share:(index + 1) * share, :] = whole[index]
    line = lax.broadcasted_iota(jnp.int32, (features, features), 0)
    column = lax.broadcasted_iota(jnp.int32, (features, features), 1)
    shared[...] = shared[...] * (slot_count / total_items) + jnp.where(
        line == column, 0.5 * slot_count, 0.0
    )

    def common(value):
        return lax.dot_general(
            value, shared[...], NT, precision=lax.Precision.HIGHEST, preferred_element_type=f32
        )

    def apply_system(vector_parts):
        unroll = min(count, 32)

        def some(index, total):
            for j in range(unroll):
                owner = index * unroll + j
                total = products(owner, vector_parts, total, scaled[owner])
            return total

        nothing = jnp.zeros((vector_parts.shape[0], features), f32)
        if unroll == count:
            return some(0, nothing)
        return lax.fori_loop(0, count // unroll, some, nothing)

    estimate = start_ref[...]
    residual = target[...] - (common(estimate) + joined(image[...]))
    direction = residual
    norm_now = jnp.sum(residual * residual, axis=1, keepdims=True)
    for step in range(CG_STEPS):
        if step < CG_STEPS - 1:
            moved = common(direction) + joined(apply_system(split(direction)))
        else:
            moved = common(direction) + apply_system(direction.astype(jnp.bfloat16))
        curvature = jnp.sum(direction * moved, axis=1, keepdims=True)
        step_len = norm_now / (curvature + 1e-06)
        estimate = estimate + step_len * direction
        residual = residual - step_len * moved
        norm_next = jnp.sum(residual * residual, axis=1, keepdims=True)
        direction = residual + norm_next / (norm_now + 1e-06) * direction
        norm_now = norm_next
    out_ref[...] = estimate


def per_device(item_table, user_rows, link_rows, link_slots, link_weights, link_counts):
    user_count, features = user_rows.shape
    slot_count = link_rows.shape[1]
    devices = lax.axis_size("rows") * lax.axis_size("table")
    capacity = user_count * slot_count // devices
    share = features // devices
    total_items = item_table.shape[0] * devices
    vmem = pl.BlockSpec(memory_space=pltpu.VMEM)
    hbm = pl.BlockSpec(memory_space=pltpu.HBM)
    dma = pltpu.SemaphoreType.DMA
    f32, bf16, i32 = jnp.float32, jnp.bfloat16, jnp.int32

    return pl.pallas_call(
        functools.partial(sweep_kernel, total_items),
        out_shape=jax.ShapeDtypeStruct((user_count, features), f32),
        in_specs=[hbm] * 6,
        out_specs=vmem,
        scratch_shapes=[
            pltpu.SMEM(link_counts.shape, i32),
            pltpu.VMEM(link_slots.shape, i32),
            pltpu.VMEM(link_rows.shape, i32),
            pltpu.VMEM(link_weights.shape, i32),
            pltpu.VMEM(user_rows.shape, f32),
            pltpu.VMEM(item_table.shape, bf16),
            pltpu.VMEM(item_table.shape, f32),
            pltpu.VMEM((devices, 1, capacity), i32),
            pltpu.VMEM((devices, 1, capacity), i32),
            pltpu.SMEM((devices, 1, capacity), i32),
            pltpu.VMEM((2, devices, 1, capacity), f32),
            pltpu.VMEM((devices, user_count, capacity), f32),
            pltpu.VMEM((capacity, features), f32),
            pltpu.VMEM((devices, capacity, features), bf16),
            pltpu.VMEM((devices, capacity, features), bf16),
            pltpu.VMEM((devices, capacity, features), bf16),
            pltpu.VMEM((devices, share, features), f32),
            pltpu.VMEM((devices, share, features), f32),
            pltpu.VMEM((share, features), f32),
            pltpu.VMEM((devices, share, features), f32),
            pltpu.VMEM((features, features), f32),
            pltpu.VMEM((2 * user_count, features), f32),
            pltpu.VMEM((user_count, features), f32),
            dma((5,)), dma, dma((devices,)),
            dma((2, devices)), dma((2, devices)), dma((2, devices)), dma((2, devices)),
        ],
        compiler_params=pltpu.CompilerParams(
            collective_id=0, has_side_effects=True, vmem_limit_bytes=VMEM_BYTES
        ),
        name="sweep",
    )(link_counts, item_table, link_slots, link_rows, link_weights, user_rows)


def solution(mesh):
    flat = P(("rows", "table"), None)
    return jax.shard_map(
        per_device,
        mesh=mesh,
        in_specs=(flat, flat, flat, flat, flat, P(("rows", "table"))),
        out_specs=flat,
        check_vma=False,
    )
```

```python
import functools

import jax
import jax.numpy as jnp
from jax import lax
from jax.experimental import pallas as pl
from jax.experimental.pallas import tpu as pltpu
from jax.sharding import PartitionSpec as P

CG_STEPS = 3
MESH = pl.DeviceIdType.MESH
VMEM_BYTES = 64 * 1024 * 1024 - 65536
NT = (((1,), (1,)), ((), ()))
TN = (((0,), (0,)), ((), ()))


def position():
    width = lax.axis_size("table")
    count = lax.axis_size("rows") * width
    return lax.axis_index("rows") * width + lax.axis_index("table"), count, width


def partner(step):
    me, count, width = position()
    away = lax.div(step + 1, 2) + lax.rem(step + 1, 2) * (count // 2)
    later, earlier = me + away, me - away
    later = jnp.where(later >= count, later - count, later)
    earlier = jnp.where(earlier < 0, earlier + count, earlier)
    return later, earlier, (lax.div(later, width), lax.rem(later, width))


def for_partners(body, first=0, last=None):
    _, count, _ = position()

    def step_body(step, carry):
        body(*partner(step))
        return carry

    lax.fori_loop(first, count - 1 if last is None else last, step_body, 0)


def split(value):
    high = value.astype(jnp.bfloat16)
    low = (value - high.astype(jnp.float32)).astype(jnp.bfloat16)
    return jnp.concatenate([high, low], axis=0)


def joined(value):
    half = value.shape[0] // 2
    return value[:half] + value[half:]


def place(slots_ref, read_parts, owners, capacity):
    users, width = slots_ref.shape
    shift = capacity.bit_length() - 1
    group = 8

    def one_group(index, total):
        at = pl.ds(pl.multiple_of(index * group, group), group)
        slots = slots_ref[at, :]
        owner, inner = slots >> shift, slots & (capacity - 1)
        parts = read_parts(index * group, at)

        def choose(user):
            pick = slice(user, user + 1)
            match = lax.broadcasted_iota(jnp.int32, (owners, width), 0) == owner[pick]
            left = jnp.concatenate([jnp.where(match, part[pick], 0.0) for part in parts], axis=0)
            hit = lax.broadcasted_iota(jnp.int32, (capacity, width), 0) == inner[pick]
            return left.astype(jnp.bfloat16), jnp.where(hit, 1.0, 0.0).astype(jnp.bfloat16)

        for user in range(0, group, 2):
            lefts, rights = zip(choose(user), choose(user + 1))
            total = total + lax.dot_general(
                jnp.concatenate(lefts, axis=1), jnp.concatenate(rights, axis=1), NT,
                preferred_element_type=jnp.float32,
            )
        return total

    total = lax.fori_loop(
        0, users // group, one_group, jnp.zeros((2 * owners, capacity), jnp.float32)
    )
    return total[:owners], total[owners:]


def gather_rows(read_index, source, target):
    group = 32

    def one_group(index, carry):
        start = index * group
        values = [source[pl.ds(read_index(start + i), 1), :] for i in range(group)]
        for i, value in enumerate(values):
            target[pl.ds(start + i, 1), :] = value
        return carry

    lax.fori_loop(0, target.shape[0] // group, one_group, 0)


def sweep_kernel(
    total_items,
    counts_hbm, table_hbm, slots_hbm, rows_hbm, weights_hbm, start_hbm, out_ref,
    counts_ref, slots_ref, rows_ref, weights_ref, start_ref, table, wide, wanted, asked, indices, placed, marks, stage, leaving, arrived, scaled,
    parts, partial, summed, whole, shared, image, target,
    input_sems, table_sem, index_sem, ask_sems, row_sems, part_sems, whole_sems,
):
    me, count, _ = position()
    users, features = start_ref.shape
    slot_count = slots_ref.shape[1]
    capacity = wanted.shape[2]
    share = features // count
    assert wide.shape[0] & (wide.shape[0] - 1) == 0
    f32 = jnp.float32

    def remote(source, landing, sems, outgoing, incoming, device):
        return pltpu.make_async_remote_copy(
            src_ref=source, dst_ref=landing,
            send_sem=sems.at[0, outgoing], recv_sem=sems.at[1, incoming],
            device_id=device, device_id_type=MESH,
        )

    def ask_copy(to, slot, device):
        return remote(wanted.at[to], asked.at[slot], ask_sems, to, slot, device)

    def row_copy(to, slot, device):
        return remote(leaving.at[to], arrived.at[slot], row_sems, to, slot, device)

    def part_copy(to, slot, device):
        return remote(parts.at[to], partial.at[slot], part_sems, to, slot, device)

    def whole_copy(to, slot, device):
        return remote(summed, whole.at[slot], whole_sems, to, slot, device)

    def finish(copy):
        def both(to, source, device):
            copy(to, source, device).wait()

        return both

    loads = [
        pltpu.make_async_copy(source, landing, input_sems.at[index])
        for index, (source, landing) in enumerate([
            (slots_hbm, slots_ref), (rows_hbm, rows_ref), (counts_hbm, counts_ref),
            (weights_hbm, weights_ref), (start_hbm, start_ref),
        ])
    ]
    for load in loads:
        load.start()
    load_table = pltpu.make_async_copy(table_hbm, table, table_sem)
    load_table.start()
    barrier = pltpu.get_barrier_semaphore()
    for_partners(
        lambda to, source, device: pl.semaphore_signal(
            barrier, inc=1, device_id=device, device_id_type=MESH
        )
    )
    for load in loads[:2]:
        load.wait()

    def row_parts(first, at):
        rows = rows_ref[at, :]
        return (rows >> 7).astype(f32), (rows & 127).astype(f32)

    high, low = place(slots_ref, row_parts, count, capacity)
    wanted[...] = (high * 128.0 + low).astype(jnp.int32)[:, None, :]
    pl.semaphore_wait(barrier, count - 1)
    for_partners(lambda to, source, device: ask_copy(to, me, device).start())
    asked[me] = wanted[me]

    chunk = 1024
    load_table.wait()

    def widen(index, carry):
        at = pl.ds(pl.multiple_of(index * chunk, chunk), chunk)
        wide[at, :] = table[at, :].astype(f32)
        return carry

    lax.fori_loop(0, table.shape[0] // chunk, widen, 0)

    def gather_block(owner):
        gather_rows(lambda i: indices[owner, 0, i] & (wide.shape[0] - 1), wide, stage)
        return stage[...].astype(jnp.bfloat16)

    def index_copy(owner):
        return pltpu.make_async_copy(asked.at[owner], indices.at[owner], index_sem.at[owner])

    def fetch_request(step):
        to, _, device = partner(step)
        ask_copy(to, to, device).wait()
        index_copy(to).start()

    def send_block(step):
        to, _, device = partner(step)
        index_copy(to).wait()
        leaving[to] = gather_block(to)
        row_copy(to, me, device).start()

    def send_ahead(step, carry):
        fetch_request(step + 1)
        send_block(step)
        return carry

    index_copy(me).start()
    fetch_request(0)
    lax.fori_loop(0, 4, send_ahead, 0)

    def gramian(index, total):
        at = pl.ds(pl.multiple_of(index * chunk, chunk), chunk)
        block = table[at, :]
        return total + lax.dot_general(block, block, TN, preferred_element_type=f32)

    own = lax.fori_loop(
        0, table.shape[0] // chunk, gramian, jnp.zeros((features, features), f32)
    )
    for index in range(count):
        parts[index] = own[index * share:(index + 1) * share]
    for_partners(lambda to, source, device: part_copy(to, me, device).start())
    partial[me] = parts[me]

    lax.fori_loop(4, count // 2, send_ahead, 0)
    for_partners(finish(part_copy))
    summed[...] = jnp.sum(partial[...], axis=0)
    for_partners(lambda to, source, device: whole_copy(to, me, device).start())
    whole[me] = summed[...]
    lax.fori_loop(count // 2, count - 2, send_ahead, 0)
    send_block(count - 2)
    index_copy(me).wait()
    arrived[me] = gather_block(me)

    for load in loads[2:]:
        load.wait()

    def link_parts(first, at):
        shape = (8, slot_count)
        line = lax.broadcasted_iota(jnp.int32, shape, 0)
        limit = jnp.zeros(shape, jnp.int32)
        for j in range(shape[0]):
            limit = jnp.where(line == j, counts_ref[first + j], limit)
        live = lax.broadcasted_iota(jnp.int32, shape, 1) < limit
        confidence = jnp.where(live, 1.0 + weights_ref[at, :].astype(f32) / 8.0, 0.0)
        return (line + first).astype(f32), confidence

    member, confidence = place(slots_ref, link_parts, count, capacity)
    placed[0] = member[:, None, :]
    placed[1] = confidence[:, None, :]

    def mark(owner, carry):
        line = lax.broadcasted_iota(jnp.int32, (users, capacity), 0)
        hit = line == placed[0, owner].astype(jnp.int32)
        marks[owner] = jnp.where(hit, placed[1, owner], 0.0)
        return carry

    lax.fori_loop(0, count, mark, 0)

    def products(owner, vector_parts, total, weighted):
        inner = lax.dot_general(vector_parts, arrived[owner], NT, preferred_element_type=f32)
        whole_parts = vector_parts.shape[0] == users
        inner = jnp.where(marks[owner] > 0.0, inner if whole_parts else joined(inner), 0.0)
        inner_parts = inner.astype(jnp.bfloat16) if whole_parts else split(inner)
        return total + jnp.dot(inner_parts, weighted, preferred_element_type=f32)

    start_parts = split(start_ref[...])
    image[...] = jnp.zeros_like(image)
    target[...] = jnp.zeros_like(target)
    ones = jnp.ones((users, features), jnp.bfloat16)

    def take_blocks(owners):
        goals, images = target[...], image[...]
        for owner in owners:
            marked = marks[owner]
            spread = lax.dot_general(
                marked.astype(jnp.bfloat16), ones, TN, preferred_element_type=f32
            )
            weighted = (spread * arrived[owner].astype(f32)).astype(jnp.bfloat16)
            scaled[owner] = weighted
            member = jnp.where(marked > 0.0, 1.0, 0.0).astype(jnp.bfloat16)
            goals = goals + jnp.dot(member, weighted, preferred_element_type=f32)
            images = products(owner, start_parts, images, weighted)
        target[...] = goals
        image[...] = images

    def receive_blocks(steps):
        sources = []
        for step in steps:
            to, source, device = partner(step)
            row_copy(to, source, device).wait()
            sources.append(source)
        take_blocks(sources)

    def receive_pair(index, carry):
        receive_blocks([2 * index + 1, 2 * index + 2])
        return carry

    take_blocks([me])
    receive_blocks([0])
    pairs = (count - 2) // 2
    lax.fori_loop(0, pairs, receive_pair, 0)
    for_partners(finish(whole_copy))

    for index in range(count):
        shared[index * share:(index + 1) * share, :] = whole[index]
    line = lax.broadcasted_iota(jnp.int32, (features, features), 0)
    column = lax.broadcasted_iota(jnp.int32, (features, features), 1)
    shared[...] = shared[...] * (slot_count / total_items) + jnp.where(
        line == column, 0.5 * slot_count, 0.0
    )

    def common(value):
        return lax.dot_general(
            value, shared[...], NT, precision=lax.Precision.HIGHEST, preferred_element_type=f32
        )

    def apply_system(vector_parts):
        unroll = min(count, 32)

        def some(index, total):
            for j in range(unroll):
                owner = index * unroll + j
                total = products(owner, vector_parts, total, scaled[owner])
            return total

        nothing = jnp.zeros((vector_parts.shape[0], features), f32)
        if unroll == count:
            return some(0, nothing)
        return lax.fori_loop(0, count // unroll, some, nothing)

    estimate = start_ref[...]
    residual = target[...] - (common(estimate) + joined(image[...]))
    direction = residual
    norm_now = jnp.sum(residual * residual, axis=1, keepdims=True)
    for step in range(CG_STEPS):
        if step < CG_STEPS - 1:
            moved = common(direction) + joined(apply_system(split(direction)))
        else:
            moved = common(direction) + apply_system(direction.astype(jnp.bfloat16))
        curvature = jnp.sum(direction * moved, axis=1, keepdims=True)
        step_len = norm_now / (curvature + 1e-06)
        estimate = estimate + step_len * direction
        residual = residual - step_len * moved
        norm_next = jnp.sum(residual * residual, axis=1, keepdims=True)
        direction = residual + norm_next / (norm_now + 1e-06) * direction
        norm_now = norm_next
    out_ref[...] = estimate


def per_device(item_table, user_rows, link_rows, link_slots, link_weights, link_counts):
    user_count, features = user_rows.shape
    slot_count = link_rows.shape[1]
    devices = lax.axis_size("rows") * lax.axis_size("table")
    capacity = user_count * slot_count // devices
    share = features // devices
    total_items = item_table.shape[0] * devices
    vmem = pl.BlockSpec(memory_space=pltpu.VMEM)
    hbm = pl.BlockSpec(memory_space=pltpu.HBM)
    dma = pltpu.SemaphoreType.DMA
    f32, bf16, i32 = jnp.float32, jnp.bfloat16, jnp.int32

    return pl.pallas_call(
        functools.partial(sweep_kernel, total_items),
        out_shape=jax.ShapeDtypeStruct((user_count, features), f32),
        in_specs=[hbm] * 6,
        out_specs=vmem,
        scratch_shapes=[
            pltpu.SMEM(link_counts.shape, i32),
            pltpu.VMEM(link_slots.shape, i32),
            pltpu.VMEM(link_rows.shape, i32),
            pltpu.VMEM(link_weights.shape, i32),
            pltpu.VMEM(user_rows.shape, f32),
            pltpu.VMEM(item_table.shape, bf16),
            pltpu.VMEM(item_table.shape, f32),
            pltpu.VMEM((devices, 1, capacity), i32),
            pltpu.VMEM((devices, 1, capacity), i32),
            pltpu.SMEM((devices, 1, capacity), i32),
            pltpu.VMEM((2, devices, 1, capacity), f32),
            pltpu.VMEM((devices, user_count, capacity), f32),
            pltpu.VMEM((capacity, features), f32),
            pltpu.VMEM((devices, capacity, features), bf16),
            pltpu.VMEM((devices, capacity, features), bf16),
            pltpu.VMEM((devices, capacity, features), bf16),
            pltpu.VMEM((devices, share, features), f32),
            pltpu.VMEM((devices, share, features), f32),
            pltpu.VMEM((share, features), f32),
            pltpu.VMEM((devices, share, features), f32),
            pltpu.VMEM((features, features), f32),
            pltpu.VMEM((2 * user_count, features), f32),
            pltpu.VMEM((user_count, features), f32),
            dma((5,)), dma, dma((devices,)),
            dma((2, devices)), dma((2, devices)), dma((2, devices)), dma((2, devices)),
        ],
        compiler_params=pltpu.CompilerParams(
            collective_id=0, has_side_effects=True, vmem_limit_bytes=VMEM_BYTES
        ),
        name="sweep",
    )(link_counts, item_table, link_slots, link_rows, link_weights, user_rows)


def solution(mesh):
    flat = P(("rows", "table"), None)
    return jax.shard_map(
        per_device,
        mesh=mesh,
        in_specs=(flat, flat, flat, flat, flat, P(("rows", "table"))),
        out_specs=flat,
        check_vma=False,
    )
```

```python
import functools

import jax
import jax.numpy as jnp
from jax import lax
from jax.experimental import pallas as pl
from jax.experimental.pallas import tpu as pltpu
from jax.sharding import PartitionSpec as P

CG_STEPS = 3
PLACED = 32
MESH = pl.DeviceIdType.MESH
VMEM_BYTES = 64 * 1024 * 1024 - 65536
NT = (((1,), (1,)), ((), ()))
TN = (((0,), (0,)), ((), ()))


def position():
    width = lax.axis_size("table")
    count = lax.axis_size("rows") * width
    return lax.axis_index("rows") * width + lax.axis_index("table"), count, width


def partner(step):
    me, count, width = position()
    away = lax.div(step + 1, 2) + lax.rem(step + 1, 2) * (count // 2)
    later, earlier = me + away, me - away
    later = jnp.where(later >= count, later - count, later)
    earlier = jnp.where(earlier < 0, earlier + count, earlier)
    return later, earlier, (lax.div(later, width), lax.rem(later, width))


def for_partners(body, first=0, last=None):
    _, count, _ = position()

    def step_body(step, carry):
        body(*partner(step))
        return carry

    lax.fori_loop(first, count - 1 if last is None else last, step_body, 0)


def split(value):
    high = value.astype(jnp.bfloat16)
    low = (value - high.astype(jnp.float32)).astype(jnp.bfloat16)
    return jnp.concatenate([high, low], axis=0)


def joined(value):
    half = value.shape[0] // 2
    return value[:half] + value[half:]


def place(slots_ref, read_parts, owners, capacity):
    users, width = slots_ref.shape
    shift = capacity.bit_length() - 1
    group = PLACED

    def one_group(index, total):
        at = pl.ds(pl.multiple_of(index * group, group), group)
        slots = slots_ref[at, :]
        owner, inner = slots >> shift, slots & (capacity - 1)
        parts = read_parts(index * group, at)

        def choose(user):
            pick = slice(user, user + 1)
            match = lax.broadcasted_iota(jnp.int32, (owners, width), 0) == owner[pick]
            left = jnp.concatenate([jnp.where(match, part[pick], 0.0) for part in parts], axis=0)
            hit = lax.broadcasted_iota(jnp.int32, (capacity, width), 0) == inner[pick]
            return left.astype(jnp.bfloat16), jnp.where(hit, 1.0, 0.0).astype(jnp.bfloat16)

        for user in range(0, group, 2):
            lefts, rights = zip(choose(user), choose(user + 1))
            total = total + lax.dot_general(
                jnp.concatenate(lefts, axis=1), jnp.concatenate(rights, axis=1), NT,
                preferred_element_type=jnp.float32,
            )
        return total

    total = lax.fori_loop(
        0, users // group, one_group, jnp.zeros((2 * owners, capacity), jnp.float32)
    )
    return total[:owners], total[owners:]


def gather_rows(read_index, source, target):
    group = 32

    def one_group(index, carry):
        start = index * group
        values = [source[pl.ds(read_index(start + i), 1), :] for i in range(group)]
        for i, value in enumerate(values):
            target[pl.ds(start + i, 1), :] = value
        return carry

    lax.fori_loop(0, target.shape[0] // group, one_group, 0)


def sweep_kernel(
    total_items,
    counts_hbm, table_hbm, slots_hbm, rows_hbm, weights_hbm, start_hbm, out_ref,
    counts_ref, slots_ref, rows_ref, weights_ref, start_ref, table, wide, wanted, asked, indices, placed, marks, stage, leaving, arrived, scaled,
    parts, partial, summed, whole, shared, image, target,
    input_sems, table_sem, index_sem, ask_sems, row_sems, part_sems, whole_sems,
):
    me, count, _ = position()
    users, features = start_ref.shape
    slot_count = slots_ref.shape[1]
    capacity = wanted.shape[2]
    share = features // count
    assert wide.shape[0] & (wide.shape[0] - 1) == 0
    f32 = jnp.float32

    def remote(source, landing, sems, outgoing, incoming, device):
        return pltpu.make_async_remote_copy(
            src_ref=source, dst_ref=landing,
            send_sem=sems.at[0, outgoing], recv_sem=sems.at[1, incoming],
            device_id=device, device_id_type=MESH,
        )

    def ask_copy(to, slot, device):
        return remote(wanted.at[to], asked.at[slot], ask_sems, to, slot, device)

    def row_copy(to, slot, device):
        return remote(leaving.at[to], arrived.at[slot], row_sems, to, slot, device)

    def part_copy(to, slot, device):
        return remote(parts.at[to], partial.at[slot], part_sems, to, slot, device)

    def whole_copy(to, slot, device):
        return remote(summed, whole.at[slot], whole_sems, to, slot, device)

    def finish(copy):
        def both(to, source, device):
            copy(to, source, device).wait()

        return both

    loads = [
        pltpu.make_async_copy(source, landing, input_sems.at[index])
        for index, (source, landing) in enumerate([
            (slots_hbm, slots_ref), (rows_hbm, rows_ref), (counts_hbm, counts_ref),
            (weights_hbm, weights_ref), (start_hbm, start_ref),
        ])
    ]
    for load in loads:
        load.start()
    load_table = pltpu.make_async_copy(table_hbm, table, table_sem)
    load_table.start()
    barrier = pltpu.get_barrier_semaphore()
    for_partners(
        lambda to, source, device: pl.semaphore_signal(
            barrier, inc=1, device_id=device, device_id_type=MESH
        )
    )
    for load in loads[:2]:
        load.wait()

    def row_parts(first, at):
        rows = rows_ref[at, :]
        return (rows >> 7).astype(f32), (rows & 127).astype(f32)

    high, low = place(slots_ref, row_parts, count, capacity)
    wanted[...] = (high * 128.0 + low).astype(jnp.int32)[:, None, :]
    pl.semaphore_wait(barrier, count - 1)
    for_partners(lambda to, source, device: ask_copy(to, me, device).start())
    asked[me] = wanted[me]

    chunk = 1024
    load_table.wait()

    def widen(index, carry):
        at = pl.ds(pl.multiple_of(index * chunk, chunk), chunk)
        wide[at, :] = table[at, :].astype(f32)
        return carry

    lax.fori_loop(0, table.shape[0] // chunk, widen, 0)

    def gather_block(owner):
        gather_rows(lambda i: indices[owner, 0, i] & (wide.shape[0] - 1), wide, stage)
        return stage[...].astype(jnp.bfloat16)

    def index_copy(owner):
        return pltpu.make_async_copy(asked.at[owner], indices.at[owner], index_sem.at[owner])

    def fetch_request(step):
        to, _, device = partner(step)
        ask_copy(to, to, device).wait()
        index_copy(to).start()

    def send_block(step):
        to, _, device = partner(step)
        index_copy(to).wait()
        leaving[to] = gather_block(to)
        row_copy(to, me, device).start()

    def send_ahead(step, carry):
        fetch_request(step + 1)
        send_block(step)
        return carry

    index_copy(me).start()
    fetch_request(0)
    lax.fori_loop(0, 4, send_ahead, 0)

    def gramian(index, total):
        at = pl.ds(pl.multiple_of(index * chunk, chunk), chunk)
        block = table[at, :]
        return total + lax.dot_general(block, block, TN, preferred_element_type=f32)

    own = lax.fori_loop(
        0, table.shape[0] // chunk, gramian, jnp.zeros((features, features), f32)
    )
    for index in range(count):
        parts[index] = own[index * share:(index + 1) * share]
    for_partners(lambda to, source, device: part_copy(to, me, device).start())
    partial[me] = parts[me]

    lax.fori_loop(4, count // 2, send_ahead, 0)
    for_partners(finish(part_copy))
    summed[...] = jnp.sum(partial[...], axis=0)
    for_partners(lambda to, source, device: whole_copy(to, me, device).start())
    whole[me] = summed[...]
    lax.fori_loop(count // 2, count - 2, send_ahead, 0)
    send_block(count - 2)
    index_copy(me).wait()
    arrived[me] = gather_block(me)

    for load in loads[2:]:
        load.wait()

    def link_parts(first, at):
        shape = (PLACED, slot_count)
        line = lax.broadcasted_iota(jnp.int32, shape, 0)
        limit = jnp.zeros(shape, jnp.int32)
        for j in range(shape[0]):
            limit = jnp.where(line == j, counts_ref[first + j], limit)
        live = lax.broadcasted_iota(jnp.int32, shape, 1) < limit
        confidence = jnp.where(live, 1.0 + weights_ref[at, :].astype(f32) / 8.0, 0.0)
        return (line + first).astype(f32), confidence

    member, confidence = place(slots_ref, link_parts, count, capacity)
    placed[0] = member[:, None, :]
    placed[1] = confidence[:, None, :]

    def mark(owner, carry):
        line = lax.broadcasted_iota(jnp.int32, (users, capacity), 0)
        hit = line == placed[0, owner].astype(jnp.int32)
        marks[owner] = jnp.where(hit, placed[1, owner], 0.0)
        return carry

    lax.fori_loop(0, count, mark, 0)

    def products(owner, vector_parts, total, weighted):
        inner = lax.dot_general(vector_parts, arrived[owner], NT, preferred_element_type=f32)
        whole_parts = vector_parts.shape[0] == users
        inner = jnp.where(marks[owner] > 0.0, inner if whole_parts else joined(inner), 0.0)
        inner_parts = inner.astype(jnp.bfloat16) if whole_parts else split(inner)
        return total + jnp.dot(inner_parts, weighted, preferred_element_type=f32)

    start_parts = split(start_ref[...])
    image[...] = jnp.zeros_like(image)
    target[...] = jnp.zeros_like(target)
    ones = jnp.ones((users, features), jnp.bfloat16)

    def take_blocks(owners):
        goals, images = target[...], image[...]
        for owner in owners:
            marked = marks[owner]
            spread = lax.dot_general(
                marked.astype(jnp.bfloat16), ones, TN, preferred_element_type=f32
            )
            weighted = (spread * arrived[owner].astype(f32)).astype(jnp.bfloat16)
            scaled[owner] = weighted
            member = jnp.where(marked > 0.0, 1.0, 0.0).astype(jnp.bfloat16)
            goals = goals + jnp.dot(member, weighted, preferred_element_type=f32)
            images = products(owner, start_parts, images, weighted)
        target[...] = goals
        image[...] = images

    def receive_blocks(steps):
        sources = []
        for step in steps:
            to, source, device = partner(step)
            row_copy(to, source, device).wait()
            sources.append(source)
        take_blocks(sources)

    def receive_pair(index, carry):
        receive_blocks([2 * index + 1, 2 * index + 2])
        return carry

    take_blocks([me])
    receive_blocks([0])
    pairs = (count - 2) // 2
    lax.fori_loop(0, pairs, receive_pair, 0)
    for_partners(finish(whole_copy))

    for index in range(count):
        shared[index * share:(index + 1) * share, :] = whole[index]
    line = lax.broadcasted_iota(jnp.int32, (features, features), 0)
    column = lax.broadcasted_iota(jnp.int32, (features, features), 1)
    shared[...] = shared[...] * (slot_count / total_items) + jnp.where(
        line == column, 0.5 * slot_count, 0.0
    )

    def common(value):
        return lax.dot_general(
            value, shared[...], NT, precision=lax.Precision.HIGHEST, preferred_element_type=f32
        )

    def apply_system(vector_parts):
        unroll = min(count, 32)

        def some(index, total):
            for j in range(unroll):
                owner = index * unroll + j
                total = products(owner, vector_parts, total, scaled[owner])
            return total

        nothing = jnp.zeros((vector_parts.shape[0], features), f32)
        if unroll == count:
            return some(0, nothing)
        return lax.fori_loop(0, count // unroll, some, nothing)

    estimate = start_ref[...]
    residual = target[...] - (common(estimate) + joined(image[...]))
    direction = residual
    norm_now = jnp.sum(residual * residual, axis=1, keepdims=True)
    for step in range(CG_STEPS):
        if step < CG_STEPS - 1:
            moved = common(direction) + joined(apply_system(split(direction)))
        else:
            moved = common(direction) + apply_system(direction.astype(jnp.bfloat16))
        curvature = jnp.sum(direction * moved, axis=1, keepdims=True)
        step_len = norm_now / (curvature + 1e-06)
        estimate = estimate + step_len * direction
        residual = residual - step_len * moved
        norm_next = jnp.sum(residual * residual, axis=1, keepdims=True)
        direction = residual + norm_next / (norm_now + 1e-06) * direction
        norm_now = norm_next
    out_ref[...] = estimate


def per_device(item_table, user_rows, link_rows, link_slots, link_weights, link_counts):
    user_count, features = user_rows.shape
    slot_count = link_rows.shape[1]
    devices = lax.axis_size("rows") * lax.axis_size("table")
    capacity = user_count * slot_count // devices
    share = features // devices
    total_items = item_table.shape[0] * devices
    vmem = pl.BlockSpec(memory_space=pltpu.VMEM)
    hbm = pl.BlockSpec(memory_space=pltpu.HBM)
    dma = pltpu.SemaphoreType.DMA
    f32, bf16, i32 = jnp.float32, jnp.bfloat16, jnp.int32

    return pl.pallas_call(
        functools.partial(sweep_kernel, total_items),
        out_shape=jax.ShapeDtypeStruct((user_count, features), f32),
        in_specs=[hbm] * 6,
        out_specs=vmem,
        scratch_shapes=[
            pltpu.SMEM(link_counts.shape, i32),
            pltpu.VMEM(link_slots.shape, i32),
            pltpu.VMEM(link_rows.shape, i32),
            pltpu.VMEM(link_weights.shape, i32),
            pltpu.VMEM(user_rows.shape, f32),
            pltpu.VMEM(item_table.shape, bf16),
            pltpu.VMEM(item_table.shape, f32),
            pltpu.VMEM((devices, 1, capacity), i32),
            pltpu.VMEM((devices, 1, capacity), i32),
            pltpu.SMEM((devices, 1, capacity), i32),
            pltpu.VMEM((2, devices, 1, capacity), f32),
            pltpu.VMEM((devices, user_count, capacity), f32),
            pltpu.VMEM((capacity, features), f32),
            pltpu.VMEM((devices, capacity, features), bf16),
            pltpu.VMEM((devices, capacity, features), bf16),
            pltpu.VMEM((devices, capacity, features), bf16),
            pltpu.VMEM((devices, share, features), f32),
            pltpu.VMEM((devices, share, features), f32),
            pltpu.VMEM((share, features), f32),
            pltpu.VMEM((devices, share, features), f32),
            pltpu.VMEM((features, features), f32),
            pltpu.VMEM((2 * user_count, features), f32),
            pltpu.VMEM((user_count, features), f32),
            dma((5,)), dma, dma((devices,)),
            dma((2, devices)), dma((2, devices)), dma((2, devices)), dma((2, devices)),
        ],
        compiler_params=pltpu.CompilerParams(
            collective_id=0, has_side_effects=True, vmem_limit_bytes=VMEM_BYTES
        ),
        name="sweep",
    )(link_counts, item_table, link_slots, link_rows, link_weights, user_rows)


def solution(mesh):
    flat = P(("rows", "table"), None)
    return jax.shard_map(
        per_device,
        mesh=mesh,
        in_specs=(flat, flat, flat, flat, flat, P(("rows", "table"))),
        out_specs=flat,
        check_vma=False,
    )
```
